512 devices in a mesh: param: 128 (over y_lo, x, z), freq: 4 (over y_hi, core).
Axes of the slice: x: 4, y: 4 (y_hi: 2, y_lo: 2; y = y_hi * 2 + y_lo), z: 16, core: 2. Of those that a mesh axis runs over, the one named last changes fastest.
Arguments:
- direction: bfloat16 [420, 8, 65536], P('freq', None, 'param'), may hold values from -6 to 6
- green_blocks: bfloat16 [8, 2, 600, 65536], P('freq', None, None, 'param'), may hold values from -0.0234375 to 0.0234375
- block_mask: int32 [8, 512], P(None, 'param'), may hold values 0 or 1
- noise_weights: float32 [8, 600], P('freq'), may hold values from 17 to 132
- prior_precision: float32 [65536], P('param'), may hold values from 0.05 to 0.5
- freq_index: int32 [8], replicated, may hold values from 1 to 209, as said below
Outputs:
- hessian_action: bfloat16 [420, 8, 65536], P('freq', None, 'param')
The draws below stay inside these ranges and needn't reach their ends.
Inputs may be any that keep to these rules, and one draw needn't show every extreme that they name: `freq_index`: distinct values.
All inputs are finite; a program needn't handle non-finite values. No bound on the sum of `block_mask` on one device may be relied on, other than what follows from the above.
Results may differ from the reference program's by a relative error of at most 0.012.
Values may be sent and summed in bfloat16 or wider, within the bound.
A program may use at most 64 MiB of HBM per device.

```python
import math
import jax
import jax.numpy as jnp
from jax import lax

SENSORS = 600
NT = 420
NF = 8
RHS = 8
SBLK = 8
PBLK = 128
PARAMS = 65536


def draw_freq_index(key, part):
    key = jax.random.fold_in(key, 7)
    highest = NT // 2 - 1
    picks = 1 + jax.random.permutation(key, highest - 1)[:NF - 1]
    full = jnp.concatenate([picks.astype(jnp.int32), jnp.full((1,), highest, jnp.int32)])
    order = jax.random.permutation(jax.random.fold_in(key, 1), NF)
    return full[order].astype(jnp.int32)


def touch_ends(drawn, stream_key, least, largest):
    extent = drawn.shape
    index_at = [jax.random.randint(jax.random.fold_in(stream_key, axis), (), 0, extent[axis]) for axis in range(len(extent))]
    drawn = drawn.at[tuple(index_at)].set(least)
    longest = extent.index(max(extent))
    index_at[longest] = (index_at[longest] + 1) % extent[longest]
    return drawn.at[tuple(index_at)].set(largest)


def block_scale(own_key, extent, cuts, low, top_value):
    gain, own = 1.0, jax.random.fold_in(own_key, 6)
    for position, blocks in cuts:
        draws = jnp.exp(jax.random.uniform(jax.random.fold_in(own, position), (blocks,), jnp.float32, low / len(cuts), top_value / len(cuts)))
        gain = gain * jnp.repeat(draws, extent[position] // blocks).reshape([-1 if axis == position else 1 for axis in range(len(extent))])
    return gain


def scatter_about(stream_key, extent, width, bound, split=(), kind=jnp.bfloat16):
    level = block_scale(stream_key, extent, split, -0.22, 0.18) if split else 1.0
    result = jax.random.normal(stream_key, extent, jnp.float32) * width * level
    return jnp.minimum(jnp.maximum(result, -bound), bound).astype(kind)


def setup_inputs(seed: int = 0) -> dict:
    seeds = jax.random.split(jax.random.key(seed), 7)
    direction = scatter_about(seeds[0], (NT, RHS, PARAMS), 1.0, 6.0, ((0, 4), (2, 128)))
    green_blocks = scatter_about(seeds[1], (NF, 2, SENSORS, PARAMS), PARAMS ** -0.5, 0.0234375, ((0, 4), (3, 128)))
    block_mask = touch_ends((jax.random.randint(seeds[2], (SBLK, PARAMS // PBLK), 0, 4) < 3).astype(jnp.int32), jax.random.fold_in(seeds[2], 1), 0, 1)
    noise_weights = jnp.clip(jnp.exp(math.log(132.0) - 2.0495886 * jax.random.uniform(seeds[3], (NF, SENSORS), jnp.float32) ** block_scale(seeds[3], (NF, SENSORS), ((0, 4),), -0.2, 0.2)), 17.0, 132.0)
    prior_precision = jnp.clip(jnp.exp(math.log(0.5) - 2.3025851 * jax.random.uniform(seeds[4], (PARAMS,), jnp.float32) ** block_scale(seeds[4], (PARAMS,), ((0, 128),), -0.2, 0.2)), 0.05, 0.5)
    freq_index = draw_freq_index(jax.random.fold_in(seeds[6], 71), 0)
    return dict(direction=direction, green_blocks=green_blocks, block_mask=block_mask, noise_weights=noise_weights, prior_precision=prior_precision, freq_index=freq_index)


def tables(freq_index, times):
    phase = freq_index[:, None] * times[None, :] % NT
    angle = phase.astype(jnp.float32) * (2.0 * math.pi / NT)
    factor = 1.0 / math.sqrt(NT)
    return jnp.stack([jnp.cos(angle) * factor, -jnp.sin(angle) * factor], axis=1).astype(jnp.bfloat16)

def expand_mask(block_mask, sensors, columns):
    blocks = block_mask.astype(jnp.bfloat16)
    grid = jnp.broadcast_to(blocks[:, None, :, None], (SBLK, sensors // SBLK, blocks.shape[1], PBLK))
    return grid.reshape(sensors, columns)

def reference(direction, green_blocks, block_mask, noise_weights, prior_precision, freq_index):
    table = tables(freq_index, jnp.arange(NT, dtype=jnp.int32))
    spectrum = jnp.einsum('wct,trp->wcrp', table.astype(jnp.float32), direction.astype(jnp.float32)).astype(jnp.bfloat16)
    masks = expand_mask(block_mask, SENSORS, PARAMS)

    def per_freq(items):
        blocks, spec, weights = items
        kernel_real = blocks[0] * masks
        kernel_imag = blocks[1] * masks
        spec_real, spec_imag = (spec[0], spec[1])
        data_real = jnp.dot(spec_real, kernel_real.T, preferred_element_type=jnp.float32) - jnp.dot(spec_imag, kernel_imag.T, preferred_element_type=jnp.float32)
        data_imag = jnp.dot(spec_real, kernel_imag.T, preferred_element_type=jnp.float32) + jnp.dot(spec_imag, kernel_real.T, preferred_element_type=jnp.float32)
        weighted_real = (data_real * weights[None, :]).astype(jnp.bfloat16)
        weighted_imag = (data_imag * weights[None, :]).astype(jnp.bfloat16)
        image_real = jnp.dot(weighted_real, kernel_real, preferred_element_type=jnp.float32) + jnp.dot(weighted_imag, kernel_imag, preferred_element_type=jnp.float32)
        image_imag = jnp.dot(weighted_imag, kernel_real, preferred_element_type=jnp.float32) - jnp.dot(weighted_real, kernel_imag, preferred_element_type=jnp.float32)
        return jnp.stack([image_real, image_imag], axis=0).astype(jnp.bfloat16)
    image = lax.map(per_freq, (green_blocks, spectrum, noise_weights))
    table_back = (2 * table).astype(jnp.float32)
    summed = jnp.einsum('wct,wcrp->trp', table_back, image.astype(jnp.float32))
    damped = prior_precision[None, None, :] * direction.astype(jnp.float32)
    return (damped + summed).astype(jnp.bfloat16)
```

```python
import functools
import math

import jax
import jax.numpy as jnp
from jax import lax
from jax.experimental import pallas as pl
from jax.experimental.pallas import tpu as pltpu
from jax.sharding import PartitionSpec as P

NT = 420
NF = 8
RHS = 8
SENSORS = 600
SBLK = 8
PBLK = 128
LANES = 128
PLANE = 8
MESH = pl.DeviceIdType.MESH
F32 = jnp.float32
BF16 = jnp.bfloat16


def trig(freq, component, time):
    turn = freq * time + component * (NT // 4)
    phase = turn - NT * jnp.floor(turn * (1.0 / NT))
    phase = jnp.where(phase < 0, phase + NT, phase)
    phase = jnp.where(phase >= NT, phase - NT, phase)
    y = (jnp.abs(phase - NT // 2) - NT // 4) * (2.0 * math.pi / NT)
    s = y * y
    poly = -1.0 / 39916800
    for coef in (1.0 / 362880, -1.0 / 5040, 1.0 / 120, -1.0 / 6, 1.0):
        poly = poly * s + coef
    return poly * y * (1.0 / math.sqrt(NT))


def expanded_table(freq_ref, first_time, rows, columns, key_axis):
    key_shape = (rows, 1) if key_axis == 0 else (1, columns)
    step_shape = (1, columns) if key_axis == 0 else (rows, 1)
    key = lax.broadcasted_iota(jnp.int32, key_shape, key_axis)
    step = lax.broadcasted_iota(jnp.int32, step_shape, 1 - key_axis)
    freq = jnp.zeros(key_shape, F32)
    for w in range(NF):
        freq = jnp.where(key // (2 * RHS) == w, freq_ref[w].astype(F32), freq)
    component = (key // RHS % 2).astype(F32)
    time = (step // RHS + first_time).astype(F32)
    values = trig(freq, component, time)
    return jnp.where(key % RHS == step % RHS, values, 0.0)


def forward_kernel(
    ring, n_freq, dir_hbm, green_hbm, mask_ref, noise_ref, freq_ref,
    image_out, back_out,
    dirs, green, kern, mask, back, noise,
    spec_own, spec_send, spec_recv, data_send, data_recv, sum_send, sum_recv, weighted, image_send,
    load_sem, local_sem,
    spec_ssem, spec_rsem, data_ssem, data_rsem, sum_ssem, sum_rsem, w_ssem, w_rsem, im_ssem, im_rsem,
):
    param = lax.axis_index("param")
    q = lax.axis_index("freq")
    k, z = param // ring, param % ring
    times = dirs.shape[0]
    columns = dirs.shape[2]
    own_w = NF // n_freq
    rows = own_w * 2 * RHS
    tiles = data_send.shape[0]
    padded = tiles * LANES

    def freq_peer(off):
        return (param, (q + off) % n_freq)

    def plane_peer(to):
        return (to * ring + z, q)

    def ring_peer(off):
        return (k * ring + (z + off) % ring, q)

    def remote(src, dst, ssem, rsem, to):
        return pltpu.make_async_remote_copy(
            src_ref=src, dst_ref=dst, send_sem=ssem, recv_sem=rsem, device_id=to, device_id_type=MESH
        )

    load_dir = pltpu.make_async_copy(dir_hbm, dirs, load_sem.at[0])
    load_dir.start()
    load_green = pltpu.make_async_copy(green_hbm, green, load_sem.at[1])
    load_green.start()

    barrier = pltpu.get_barrier_semaphore()
    peers = [freq_peer(o) for o in range(1, n_freq)]
    peers += [plane_peer((k + o) % PLANE) for o in range(1, PLANE)]
    peers += [ring_peer(o) for o in range(1, ring)]
    for peer in peers:
        pl.semaphore_signal(barrier, inc=1, device_id=peer, device_id_type=MESH)

    table = expanded_table(freq_ref, q * times, NF * 2 * RHS, times * RHS, 0).astype(BF16)
    load_dir.wait()
    steps = dirs[...].astype(F32).reshape(times * RHS, columns).astype(BF16)
    part = jnp.dot(table, steps, preferred_element_type=F32)
    for g in range(n_freq):
        piece = part[g * rows : (g + 1) * rows]
        spec_own[g] = piece
        spec_send[g] = piece.astype(BF16)

    pl.semaphore_wait(barrier, len(peers))
    spec_copies = []
    for off in range(1, n_freq):
        copy = remote(
            spec_send.at[(q + off) % n_freq], spec_recv.at[off - 1], spec_ssem.at[off - 1], spec_rsem.at[off - 1],
            freq_peer(off),
        )
        copy.start()
        spec_copies.append(copy)

    sensor = lax.broadcasted_iota(jnp.int32, (padded, SBLK), 0)
    block = lax.broadcasted_iota(jnp.int32, (padded, SBLK), 1)
    per = SENSORS // SBLK
    picks = jnp.where((sensor >= block * per) & (sensor < (block + 1) * per), 1.0, 0.0).astype(BF16)
    block8 = lax.broadcasted_iota(jnp.int32, (SBLK, LANES), 0)
    parts = []
    for b in range(columns // PBLK):
        value = jnp.zeros((SBLK, LANES), F32)
        for s in range(SBLK):
            value = jnp.where(block8 == s, mask_ref[b, s].astype(F32), value)
        parts.append(value)
    blocks = jnp.concatenate(parts, axis=1).astype(BF16)
    mask[...] = jnp.dot(picks, blocks, preferred_element_type=F32).astype(BF16)
    load_green.wait()
    for w in range(own_w):
        for c in range(2):
            kern[w, c, :SENSORS, :] = green[w, c] * mask[:SENSORS, :]
            kern[w, c, SENSORS:, :] = jnp.zeros((padded - SENSORS, columns), BF16)
    noise[...] = jnp.zeros_like(noise)
    for j in range(tiles):
        width = min(LANES, SENSORS - j * LANES)
        noise[j, :, :width] = noise_ref[:, j * LANES : j * LANES + width]

    total = spec_own[q]
    for off, copy in enumerate(spec_copies):
        copy.wait_recv()
        total = total + spec_recv[off].astype(F32)

    for w in range(own_w):
        first = total[w * 2 * RHS : (w + 1) * 2 * RHS]
        second = jnp.concatenate([-first[RHS:], first[:RHS]], axis=0)
        data = lax.dot_general(
            first.astype(BF16), kern[w, 0], (((1,), (1,)), ((), ())), preferred_element_type=F32
        ) + lax.dot_general(
            second.astype(BF16), kern[w, 1], (((1,), (1,)), ((), ())), preferred_element_type=F32
        )
        data = data.astype(BF16)
        for j in range(tiles):
            data_send[j, w * 2 * RHS : (w + 1) * 2 * RHS, :] = data[:, j * LANES : (j + 1) * LANES]

    def data_copy(off):
        to = (k + off) % PLANE
        return to, remote(
            data_send.at[to % tiles], data_recv.at[off - 1], data_ssem.at[off - 1], data_rsem.at[off - 1], plane_peer(to)
        )

    def sum_copy(off):
        return remote(sum_send, sum_recv.at[off - 1], sum_ssem.at[off - 1], sum_rsem.at[off - 1], ring_peer(off))

    def weighted_copy(off):
        own = k % tiles
        return remote(
            weighted.at[own], weighted.at[own], w_ssem.at[off - 1], w_rsem.at[own], plane_peer((k + off) % PLANE)
        )

    for off in range(1, PLANE):
        to, copy = data_copy(off)
        pl.when(to < tiles)(copy.start)

    back[...] = (
        (2.0 * expanded_table(freq_ref, q * times, times * RHS, NF * 2 * RHS, 1))
        .reshape(times, RHS, NF * 2 * RHS)
        .astype(BF16)
    )
    store_back = pltpu.make_async_copy(back, back_out, local_sem.at[0])
    store_back.start()

    @pl.when(k < tiles)
    def _():
        own = k % tiles
        acc = data_send[own].astype(F32)
        for off in range(1, PLANE):
            data_copy(off)[1].wait_recv()
            acc = acc + data_recv[off - 1].astype(F32)
        sum_send[...] = acc.astype(BF16)
        for off in range(1, ring):
            sum_copy(off).start()
        for off in range(1, ring):
            sum_copy(off).wait_recv()
            acc = acc + sum_recv[off - 1].astype(F32)
        scale = noise[own]
        scaled = [acc[w * 2 * RHS : (w + 1) * 2 * RHS] * scale[w : w + 1] for w in range(own_w)]
        weighted[own] = jnp.concatenate(scaled, axis=0).astype(BF16)
        for off in range(1, PLANE):
            weighted_copy(off).start()

    for j in range(tiles):
        arrival = remote(weighted.at[j], weighted.at[j], w_ssem.at[0], w_rsem.at[j], plane_peer((k + 1) % PLANE))
        pl.when(k != j)(arrival.wait_recv)

    for w in range(own_w):
        here = slice(w * 2 * RHS, (w + 1) * 2 * RHS)
        first = jnp.concatenate([weighted[j, here, :] for j in range(tiles)], axis=1)
        wide = first.astype(F32)
        second = jnp.concatenate([wide[RHS:], -wide[:RHS]], axis=0).astype(BF16)
        image = jnp.dot(first, kern[w, 0], preferred_element_type=F32) + jnp.dot(
            second, kern[w, 1], preferred_element_type=F32
        )
        image_send[here, :] = image.astype(BF16)

    image_copies = []
    for off in range(1, n_freq):
        copy = remote(image_send, image_out.at[q], im_ssem.at[off - 1], im_rsem.at[off - 1], freq_peer(off))
        copy.start()
        image_copies.append(copy)
    keep = pltpu.make_async_copy(image_send, image_out.at[q], local_sem.at[1])
    keep.start()

    for copy in spec_copies:
        copy.wait_send()
    for off in range(1, PLANE):
        to, copy = data_copy(off)
        pl.when(to < tiles)(copy.wait_send)

    @pl.when(k < tiles)
    def _():
        for off in range(1, ring):
            sum_copy(off).wait_send()
        for off in range(1, PLANE):
            weighted_copy(off).wait_send()

    store_back.wait()
    keep.wait()
    for copy in image_copies:
        copy.wait()


def back_kernel(table_ref, image_ref, prior_ref, dir_ref, out_ref):
    times, _, keys = table_ref.shape
    columns = dir_ref.shape[2]
    table = table_ref[...].astype(F32).reshape(times * RHS, keys).astype(BF16)
    summed = jnp.dot(table, image_ref[...], preferred_element_type=F32)
    damped = dir_ref[...].astype(F32).reshape(times * RHS, columns) * prior_ref[...]
    out_ref[...] = (summed + damped).reshape(times, RHS, columns).astype(BF16)


def on_device(ring, n_freq, direction, green_blocks, block_mask, noise_weights, prior_precision, freq_index):
    times, _, columns = direction.shape
    own_w = NF // n_freq
    rows = own_w * 2 * RHS
    keys = NF * 2 * RHS
    tiles = -(-SENSORS // LANES)
    padded = tiles * LANES
    vmem = pltpu.VMEM
    dma = pltpu.SemaphoreType.DMA
    anywhere = pl.BlockSpec(memory_space=pl.ANY)
    images, back = pl.pallas_call(
        functools.partial(forward_kernel, ring, n_freq),
        out_shape=(
            jax.ShapeDtypeStruct((n_freq, rows, columns), BF16),
            jax.ShapeDtypeStruct((times, RHS, keys), BF16),
        ),
        in_specs=[
            anywhere,
            anywhere,
            pl.BlockSpec(memory_space=pltpu.SMEM),
            pl.BlockSpec(memory_space=pltpu.VMEM),
            pl.BlockSpec(memory_space=pltpu.SMEM),
        ],
        out_specs=(anywhere, anywhere),
        scratch_shapes=[
            vmem((times, RHS, columns), BF16),
            vmem((own_w, 2, SENSORS, columns), BF16),
            vmem((own_w, 2, padded, columns), BF16),
            vmem((padded, columns), BF16),
            vmem((times, RHS, keys), BF16),
            vmem((tiles, own_w, LANES), F32),
            vmem((n_freq, rows, columns), F32),
            vmem((n_freq, rows, columns), BF16),
            vmem((n_freq - 1, rows, columns), BF16),
            vmem((tiles, rows, LANES), BF16),
            vmem((PLANE - 1, rows, LANES), BF16),
            vmem((rows, LANES), BF16),
            vmem((ring - 1, rows, LANES), BF16),
            vmem((tiles, rows, LANES), BF16),
            vmem((rows, columns), BF16),
            dma((2,)),
            dma((2,)),
            dma((n_freq - 1,)),
            dma((n_freq - 1,)),
            dma((PLANE - 1,)),
            dma((PLANE - 1,)),
            dma((ring - 1,)),
            dma((ring - 1,)),
            dma((PLANE - 1,)),
            dma((tiles,)),
            dma((n_freq - 1,)),
            dma((n_freq - 1,)),
        ],
        compiler_params=pltpu.CompilerParams(
            collective_id=0, has_side_effects=True, vmem_limit_bytes=32 * 1024 * 1024
        ),
        name="forward",
    )(direction, green_blocks, block_mask.T, noise_weights, freq_index)

    chunk = times // 3
    return pl.pallas_call(
        back_kernel,
        grid=(times // chunk,),
        out_shape=jax.ShapeDtypeStruct(direction.shape, BF16),
        in_specs=[
            pl.BlockSpec((chunk, RHS, keys), lambda i: (i, 0, 0)),
            pl.BlockSpec((keys, columns), lambda i: (0, 0)),
            pl.BlockSpec((1, columns), lambda i: (0, 0)),
            pl.BlockSpec((chunk, RHS, columns), lambda i: (i, 0, 0)),
        ],
        out_specs=pl.BlockSpec((chunk, RHS, columns), lambda i: (i, 0, 0)),
        compiler_params=pltpu.CompilerParams(vmem_limit_bytes=16 * 1024 * 1024),
        name="backward",
    )(back, images.reshape(keys, columns), prior_precision.reshape(1, columns), direction)


def solution(mesh):
    n_freq = mesh.shape["freq"]
    ring = mesh.shape["param"] // PLANE
    placed = (
        P("freq", None, "param"),
        P("freq", None, None, "param"),
        P(None, "param"),
        P("freq", None),
        P("param"),
        P(),
    )
    return jax.shard_map(
        functools.partial(on_device, ring, n_freq),
        mesh=mesh,
        in_specs=placed,
        out_specs=P("freq", None, "param"),
        check_vma=False,
    )
```

```python
import functools
import math

import jax
import jax.numpy as jnp
from jax import lax
from jax.experimental import pallas as pl
from jax.experimental.pallas import tpu as pltpu
from jax.sharding import PartitionSpec as P

NT = 420
NF = 8
RHS = 8
SENSORS = 600
SBLK = 8
PBLK = 128
LANES = 128
PLANE = 8
MESH = pl.DeviceIdType.MESH
F32 = jnp.float32
BF16 = jnp.bfloat16


def trig(freq, component, time):
    turn = freq * time + component * (NT // 4)
    phase = turn - NT * jnp.floor(turn * (1.0 / NT))
    phase = jnp.where(phase < 0, phase + NT, phase)
    phase = jnp.where(phase >= NT, phase - NT, phase)
    y = (jnp.abs(phase - NT // 2) - NT // 4) * (2.0 * math.pi / NT)
    s = y * y
    poly = -1.0 / 39916800
    for coef in (1.0 / 362880, -1.0 / 5040, 1.0 / 120, -1.0 / 6, 1.0):
        poly = poly * s + coef
    return poly * y * (1.0 / math.sqrt(NT))


def expanded_table(freq_ref, first_time, rows, columns, key_axis):
    key_shape = (rows, 1) if key_axis == 0 else (1, columns)
    step_shape = (1, columns) if key_axis == 0 else (rows, 1)
    key = lax.broadcasted_iota(jnp.int32, key_shape, key_axis)
    step = lax.broadcasted_iota(jnp.int32, step_shape, 1 - key_axis)
    freq = jnp.zeros(key_shape, F32)
    for w in range(NF):
        freq = jnp.where(key // (2 * RHS) == w, freq_ref[w].astype(F32), freq)
    component = (key // RHS % 2).astype(F32)
    time = (step // RHS + first_time).astype(F32)
    values = trig(freq, component, time)
    return jnp.where(key % RHS == step % RHS, values, 0.0)


def forward_kernel(
    ring, n_freq, dir_hbm, green_hbm, mask_hbm, noise_hbm, freq_hbm,
    image_out,
    dirs, green, mask_ref, noise_ref, freq_ref, kern, mask, noise,
    spec_own, spec_send, spec_recv, data_send, data_recv, sum_own, sum_send, sum_recv, weighted, image_send,
    load_sem, local_sem, near_sem,
    spec_ssem, spec_rsem, data_ssem, data_rsem, more_ssem, more_rsem, sum_ssem, sum_rsem, w_ssem, w_rsem, im_ssem, im_rsem,
):
    param = lax.axis_index("param")
    q = lax.axis_index("freq")
    k, z = param // ring, param % ring
    core = q % 2
    times = dirs.shape[0]
    columns = dirs.shape[2]
    own_w = NF // n_freq
    pair = 2 * RHS
    rows = own_w * pair
    units = data_send.shape[0]
    tiles = units // own_w
    padded = tiles * LANES
    extra = units - PLANE
    has_extra = k // extra == core
    second_unit = PLANE + k % extra

    def freq_peer(off):
        return (param, (q + off) % n_freq)

    def plane_peer(to):
        return (to * ring + z, q)

    def ring_peer(off):
        return (k * ring + (z + off) % ring, q)

    def remote(src, dst, ssem, rsem, to):
        return pltpu.make_async_remote_copy(
            src_ref=src, dst_ref=dst, send_sem=ssem, recv_sem=rsem, device_id=to, device_id_type=MESH
        )

    def signal(semaphore, to):
        pl.semaphore_signal(semaphore, inc=1, device_id=to, device_id_type=MESH)

    load_freq, load_dir, load_mask, load_noise, load_green = [
        pltpu.make_async_copy(src, dst, load_sem.at[i])
        for i, (src, dst) in enumerate(
            ((freq_hbm, freq_ref), (dir_hbm, dirs), (mask_hbm, mask_ref), (noise_hbm, noise_ref), (green_hbm, green))
        )
    ]
    for load in (load_freq, load_dir, load_mask, load_noise, load_green):
        load.start()

    barrier = pltpu.get_barrier_semaphore()
    peers = [plane_peer((k + o) % PLANE) for o in range(1, PLANE)]
    peers += [freq_peer(o) for o in range(1, n_freq)]
    peers += [ring_peer(1), ring_peer(ring - 1)]
    for peer in peers:
        signal(barrier, peer)
    reaches = [d for d in (1, 2, 4, 8, 16) if 2 * d <= ring // 2]

    def reach_signal(i):
        signal(near_sem.at[i], ring_peer(reaches[i]))
        signal(near_sem.at[i], ring_peer(ring - reaches[i]))

    load_freq.wait()
    table = expanded_table(freq_ref, q * times, NF * pair, times * RHS, 0).astype(BF16)
    load_dir.wait()
    steps = dirs[...].astype(F32).reshape(times * RHS, columns).astype(BF16)
    part = jnp.dot(table, steps, preferred_element_type=F32)
    for g in range(n_freq):
        piece = part[g * rows : (g + 1) * rows]
        spec_own[g] = piece
        spec_send[g] = piece.astype(BF16)

    pl.semaphore_wait(barrier, len(peers))
    spec_copies = []
    for off in (2, 3, 1) if n_freq == 4 else range(1, n_freq):
        copy = remote(
            spec_send.at[(q + off) % n_freq], spec_recv.at[off - 1], spec_ssem.at[off - 1], spec_rsem.at[off - 1],
            freq_peer(off),
        )
        copy.start()
        spec_copies.append(copy)
    if reaches:
        reach_signal(0)

    load_mask.wait()
    sensor = lax.broadcasted_iota(jnp.int32, (padded, SBLK), 0)
    block = lax.broadcasted_iota(jnp.int32, (padded, SBLK), 1)
    per = SENSORS // SBLK
    picks = jnp.where((sensor >= block * per) & (sensor < (block + 1) * per), 1.0, 0.0).astype(BF16)
    block8 = lax.broadcasted_iota(jnp.int32, (SBLK, LANES), 0)
    parts = []
    for b in range(columns // PBLK):
        value = jnp.zeros((SBLK, LANES), F32)
        for s in range(SBLK):
            value = jnp.where(block8 == s, mask_ref[b, s].astype(F32), value)
        parts.append(value)
    blocks = jnp.concatenate(parts, axis=1).astype(BF16)
    mask[...] = jnp.dot(picks, blocks, preferred_element_type=F32).astype(BF16)
    load_green.wait()
    for w in range(own_w):
        for c in range(2):
            kern[w, c, :SENSORS, :] = green[w, c] * mask[:SENSORS, :]
            kern[w, c, SENSORS:, :] = jnp.zeros((padded - SENSORS, columns), BF16)
    if reaches:
        pl.semaphore_wait(near_sem.at[0], 2)
    if len(reaches) > 1:
        reach_signal(1)
    load_noise.wait()
    noise[...] = jnp.zeros_like(noise)
    for u in range(units):
        w, j = u // tiles, u % tiles
        width = min(LANES, SENSORS - j * LANES)
        noise[u, :, :width] = jnp.broadcast_to(noise_ref[w : w + 1, j * LANES : j * LANES + width], (pair, width))

    total = spec_own[q]
    for off, copy in zip((2, 3, 1) if n_freq == 4 else range(1, n_freq), spec_copies):
        copy.wait_recv()
        total = total + spec_recv[off - 1].astype(F32)

    for w in range(own_w):
        first = total[w * pair : (w + 1) * pair]
        second = jnp.concatenate([-first[RHS:], first[:RHS]], axis=0)
        data = lax.dot_general(
            first.astype(BF16), kern[w, 0], (((1,), (1,)), ((), ())), preferred_element_type=F32
        ) + lax.dot_general(
            second.astype(BF16), kern[w, 1], (((1,), (1,)), ((), ())), preferred_element_type=F32
        )
        data = data.astype(BF16)
        for j in range(tiles):
            data_send[w * tiles + j] = data[:, j * LANES : (j + 1) * LANES]

    def data_copy(off):
        to = (k + off) % PLANE
        return remote(data_send.at[to], data_recv.at[off, 0], data_ssem.at[off], data_rsem.at[off], plane_peer(to))

    def more_copy(j):
        to = extra * core + j
        off = (to - k + PLANE) % PLANE
        return to, remote(
            data_send.at[PLANE + j], data_recv.at[off, 1], more_ssem.at[j], more_rsem.at[off], plane_peer(to)
        )

    def more_arrival(off):
        return remote(
            data_send.at[0], data_recv.at[off, 1], more_ssem.at[0], more_rsem.at[off], plane_peer((k + off) % PLANE)
        )

    def sum_copy(off, count):
        here = pl.ds(0, count)
        return remote(sum_send.at[here], sum_recv.at[off, here], sum_ssem.at[off], sum_rsem.at[off], ring_peer(off))

    def weighted_copy(off, n, unit):
        return remote(
            weighted.at[unit], weighted.at[unit], w_ssem.at[n, off], w_rsem.at[unit], plane_peer((k + off) % PLANE)
        )

    far_plane = [off for off in (6, 2, 5, 7, 3, 1, 4)]
    far_ring = sorted(range(1, ring), key=lambda off: -min(off, ring - off))

    for j in range(extra):
        to, copy = more_copy(j)
        pl.when(k != to)(copy.start)
    for off in far_plane:
        data_copy(off).start()
    if len(reaches) > 1:
        pl.semaphore_wait(near_sem.at[1], 2)
    if len(reaches) > 2:
        reach_signal(2)

    acc = data_send[k].astype(F32)
    for off in reversed(far_plane):
        data_copy(off).wait_recv()
        acc = acc + data_recv[off, 0].astype(F32)
    sum_own[0] = acc
    sum_send[0] = acc.astype(BF16)
    if len(reaches) > 2:
        pl.semaphore_wait(near_sem.at[2], 2)

    @pl.when(has_extra)
    def _():
        acc = data_send[second_unit].astype(F32)
        for off in reversed(far_plane):
            more_arrival(off).wait_recv()
            acc = acc + data_recv[off, 1].astype(F32)
        sum_own[1] = acc
        sum_send[1] = acc.astype(BF16)
        for off in far_ring:
            sum_copy(off, 2).start()
        acc = sum_own[...]
        for off in reversed(far_ring):
            sum_copy(off, 2).wait_recv()
            acc = acc + sum_recv[off].astype(F32)
        weighted[k] = (acc[0] * noise[k]).astype(BF16)
        weighted[second_unit] = (acc[1] * noise[second_unit]).astype(BF16)
        for off in far_plane:
            weighted_copy(off, 0, k).start()
            weighted_copy(off, 1, second_unit).start()

    @pl.when(jnp.logical_not(has_extra))
    def _():
        for off in far_ring:
            sum_copy(off, 1).start()
        acc = sum_own[0]
        for off in reversed(far_ring):
            sum_copy(off, 1).wait_recv()
            acc = acc + sum_recv[off, 0].astype(F32)
        weighted[k] = (acc * noise[k]).astype(BF16)
        for off in far_plane:
            weighted_copy(off, 0, k).start()

    for u in range(units):
        owner = u if u < PLANE else extra * core + u - PLANE
        arrival = remote(weighted.at[u], weighted.at[u], w_ssem.at[0, 0], w_rsem.at[u], plane_peer((k + 1) % PLANE))
        pl.when(k != owner)(arrival.wait_recv)

    for w in range(own_w):
        here = slice(w * pair, (w + 1) * pair)
        first = jnp.concatenate([weighted[w * tiles + j] for j in range(tiles)], axis=1)
        wide = first.astype(F32)
        second = jnp.concatenate([wide[RHS:], -wide[:RHS]], axis=0).astype(BF16)
        image = jnp.dot(first, kern[w, 0], preferred_element_type=F32) + jnp.dot(
            second, kern[w, 1], preferred_element_type=F32
        )
        image_send[here, :] = image.astype(BF16)

    image_copies = []
    for off in (2, 3, 1) if n_freq == 4 else range(1, n_freq):
        copy = remote(image_send, image_out.at[q], im_ssem.at[off - 1], im_rsem.at[off - 1], freq_peer(off))
        copy.start()
        image_copies.append(copy)
    keep = pltpu.make_async_copy(image_send, image_out.at[q], local_sem.at[0])
    keep.start()

    for copy in spec_copies:
        copy.wait_send()
    for j in range(extra):
        to, copy = more_copy(j)
        pl.when(k != to)(copy.wait_send)
    for off in far_plane:
        data_copy(off).wait_send()
        weighted_copy(off, 0, k).wait_send()

    @pl.when(has_extra)
    def _():
        for off in far_ring:
            sum_copy(off, 2).wait_send()
        for off in far_plane:
            weighted_copy(off, 1, second_unit).wait_send()

    @pl.when(jnp.logical_not(has_extra))
    def _():
        for off in far_ring:
            sum_copy(off, 1).wait_send()

    keep.wait()
    for copy in image_copies:
        copy.wait()


def back_kernel(
    image_hbm, prior_hbm, dir_hbm, freq_hbm, out_hbm, image, prior, dirs, outs, freq_ref, load_sem, dir_sem, out_sem
):
    times, _, columns = dirs.shape
    chunks = dir_sem.shape[0]
    size = times // chunks
    keys = image.shape[0]
    first_time = lax.axis_index("freq") * times
    load_freq = pltpu.make_async_copy(freq_hbm, freq_ref, load_sem.at[0])
    load_image = pltpu.make_async_copy(image_hbm, image, load_sem.at[1])
    load_prior = pltpu.make_async_copy(prior_hbm, prior, load_sem.at[2])
    loads, stores = [], []
    for i in range(chunks):
        here = pl.ds(i * size, size)
        loads.append(pltpu.make_async_copy(dir_hbm.at[here], dirs.at[here], dir_sem.at[i]))
        stores.append(pltpu.make_async_copy(outs.at[here], out_hbm.at[here], out_sem.at[i]))
    for load in [load_freq, load_image, load_prior] + loads:
        load.start()
    load_freq.wait()
    tables = [
        (2.0 * expanded_table(freq_ref, first_time + i * size, size * RHS, keys, 1)).astype(BF16) for i in range(chunks)
    ]
    load_prior.wait()
    load_image.wait()
    for i in range(chunks):
        here = slice(i * size, (i + 1) * size)
        summed = jnp.dot(tables[i], image[...], preferred_element_type=F32)
        loads[i].wait()
        damped = dirs[here].astype(F32).reshape(size * RHS, columns) * prior[...]
        outs[here] = (summed + damped).reshape(size, RHS, columns).astype(BF16)
        stores[i].start()
    for store in stores:
        store.wait()


def on_device(ring, n_freq, direction, green_blocks, block_mask, noise_weights, prior_precision, freq_index):
    times, _, columns = direction.shape
    own_w = NF // n_freq
    pair = 2 * RHS
    rows = own_w * pair
    keys = NF * pair
    tiles = -(-SENSORS // LANES)
    units = own_w * tiles
    padded = tiles * LANES
    vmem = pltpu.VMEM
    dma = pltpu.SemaphoreType.DMA
    anywhere = pl.BlockSpec(memory_space=pl.ANY)
    images = pl.pallas_call(
        functools.partial(forward_kernel, ring, n_freq),
        out_shape=jax.ShapeDtypeStruct((n_freq, rows, columns), BF16),
        in_specs=[anywhere] * 5,
        out_specs=anywhere,
        scratch_shapes=[
            vmem((times, RHS, columns), BF16),
            vmem((own_w, 2, SENSORS, columns), BF16),
            pltpu.SMEM(block_mask.shape[::-1], jnp.int32),
            vmem((own_w, SENSORS), F32),
            pltpu.SMEM((NF,), jnp.int32),
            vmem((own_w, 2, padded, columns), BF16),
            vmem((padded, columns), BF16),
            vmem((units, pair, LANES), F32),
            vmem((n_freq, rows, columns), F32),
            vmem((n_freq, rows, columns), BF16),
            vmem((n_freq - 1, rows, columns), BF16),
            vmem((units, pair, LANES), BF16),
            vmem((PLANE, 2, pair, LANES), BF16),
            vmem((2, pair, LANES), F32),
            vmem((2, pair, LANES), BF16),
            vmem((ring, 2, pair, LANES), BF16),
            vmem((units, pair, LANES), BF16),
            vmem((rows, columns), BF16),
            dma((5,)),
            dma((1,)),
            pltpu.SemaphoreType.REGULAR((4,)),
            dma((n_freq - 1,)),
            dma((n_freq - 1,)),
            dma((PLANE,)),
            dma((PLANE,)),
            dma((2,)),
            dma((PLANE,)),
            dma((ring,)),
            dma((ring,)),
            dma((2, PLANE)),
            dma((units,)),
            dma((n_freq - 1,)),
            dma((n_freq - 1,)),
        ],
        compiler_params=pltpu.CompilerParams(
            collective_id=0, has_side_effects=True, vmem_limit_bytes=56 * 1024 * 1024
        ),
        name="forward",
    )(direction, green_blocks, block_mask.T, noise_weights, freq_index)

    chunks = 5
    return pl.pallas_call(
        back_kernel,
        out_shape=jax.ShapeDtypeStruct(direction.shape, BF16),
        in_specs=[anywhere] * 4,
        out_specs=anywhere,
        scratch_shapes=[
            vmem((keys, columns), BF16),
            vmem((1, columns), F32),
            vmem(direction.shape, BF16),
            vmem(direction.shape, BF16),
            pltpu.SMEM((NF,), jnp.int32),
            dma((3,)),
            dma((chunks,)),
            dma((chunks,)),
        ],
        compiler_params=pltpu.CompilerParams(vmem_limit_bytes=56 * 1024 * 1024),
        name="backward",
    )(images.reshape(keys, columns), prior_precision.reshape(1, columns), direction, freq_index)


def solution(mesh):
    n_freq = mesh.shape["freq"]
    ring = mesh.shape["param"] // PLANE
    placed = (
        P("freq", None, "param"),
        P("freq", None, None, "param"),
        P(None, "param"),
        P("freq", None),
        P("param"),
        P(),
    )
    return jax.shard_map(
        functools.partial(on_device, ring, n_freq),
        mesh=mesh,
        in_specs=placed,
        out_specs=P("freq", None, "param"),
        check_vma=False,
    )
```

```python
import functools
import math

import jax
import jax.numpy as jnp
from jax import lax
from jax.experimental import pallas as pl
from jax.experimental.pallas import tpu as pltpu
from jax.sharding import PartitionSpec as P

NT = 420
NF = 8
RHS = 8
SENSORS = 600
SBLK = 8
PBLK = 128
LANES = 128
PLANE = 8
ROW = 4
MESH = pl.DeviceIdType.MESH
F32 = jnp.float32
BF16 = jnp.bfloat16


def trig(freq, component, time):
    turn = freq * time + component * (NT // 4)
    phase = turn - NT * jnp.floor(turn * (1.0 / NT))
    phase = jnp.where(phase < 0, phase + NT, phase)
    phase = jnp.where(phase >= NT, phase - NT, phase)
    y = (jnp.abs(phase - NT // 2) - NT // 4) * (2.0 * math.pi / NT)
    s = y * y
    poly = -1.0 / 39916800
    for coef in (1.0 / 362880, -1.0 / 5040, 1.0 / 120, -1.0 / 6, 1.0):
        poly = poly * s + coef
    return poly * y * (1.0 / math.sqrt(NT))


def expanded_table(freq_ref, first_time, rows, columns, key_axis):
    key_shape = (rows, 1) if key_axis == 0 else (1, columns)
    step_shape = (1, columns) if key_axis == 0 else (rows, 1)
    key = lax.broadcasted_iota(jnp.int32, key_shape, key_axis)
    step = lax.broadcasted_iota(jnp.int32, step_shape, 1 - key_axis)
    freq = jnp.zeros(key_shape, F32)
    for w in range(NF):
        freq = jnp.where(key // (2 * RHS) == w, freq_ref[w].astype(F32), freq)
    component = (key // RHS % 2).astype(F32)
    time = (step // RHS + first_time).astype(F32)
    values = trig(freq, component, time)
    return jnp.where(key % RHS == step % RHS, values, 0.0)


def forward_kernel(
    ring, n_freq, dir_hbm, green_hbm, mask_hbm, noise_hbm, freq_hbm, prior_hbm,
    out_ref,
    dirs, green, mask_ref, noise_ref, freq_ref, prior_ref, kern, turned, mask, noise,
    spec_own, spec_send, spec_recv, data_send, data_recv, sum_send, sum_recv, weighted, image_send, images, back, damped,
    load_sem, dir_sem, near_sem,
    spec_ssem, spec_rsem, data_ssem, data_rsem, sum_ssem, sum_rsem, w_ssem, w_rsem, im_ssem, im_rsem,
):
    param = lax.axis_index("param")
    q = lax.axis_index("freq")
    k, z = param // ring, param % ring
    core = q % 2
    times = dirs.shape[0]
    columns = dirs.shape[2]
    own_w = NF // n_freq
    pair = 2 * RHS
    rows = own_w * pair
    tiles = -(-SENSORS // LANES)
    units = own_w * tiles
    padded = tiles * LANES
    extra = units - PLANE
    has_extra = k // extra == core

    def place(u):
        return (u, 0) if u < PLANE else (extra * core + u - PLANE, 1)

    def freq_peer(off):
        return (param, (q + off) % n_freq)

    def plane_peer(to):
        return (to * ring + z, q)

    def ring_peer(off):
        return (k * ring + (z + off) % ring, q)

    def remote(src, dst, ssem, rsem, to):
        return pltpu.make_async_remote_copy(
            src_ref=src, dst_ref=dst, send_sem=ssem, recv_sem=rsem, device_id=to, device_id_type=MESH
        )

    def signal(semaphore, to):
        pl.semaphore_signal(semaphore, inc=1, device_id=to, device_id_type=MESH)

    load_freq, load_mask, load_noise, load_prior, load_green = [
        pltpu.make_async_copy(src, dst, load_sem.at[i])
        for i, (src, dst) in enumerate(
            (
                (freq_hbm, freq_ref), (mask_hbm, mask_ref), (noise_hbm, noise_ref), (prior_hbm, prior_ref),
                (green_hbm, green),
            )
        )
    ]
    chunks = dir_sem.shape[0]
    size = times // chunks
    load_dirs = [
        pltpu.make_async_copy(dir_hbm.at[pl.ds(i * size, size)], dirs.at[pl.ds(i * size, size)], dir_sem.at[i])
        for i in range(chunks)
    ]
    for load in [load_freq] + load_dirs:
        load.start()

    y, x = k // ROW, k % ROW
    beside = [plane_peer(y * ROW + (x + 1) % ROW), plane_peer(y * ROW + (x + ROW - 1) % ROW)]
    across = [plane_peer((y + 1) % (PLANE // ROW) * ROW + x)]

    def along(d):
        return [ring_peer(d), ring_peer(ring - d)]

    barrier = pltpu.get_barrier_semaphore()
    peers = [freq_peer(o) for o in range(1, n_freq)] + beside + across + along(1)
    for peer in peers:
        signal(barrier, peer)
    rounds = [beside + across + along(1), beside + along(2), along(4)]

    def tell(i):
        for peer in rounds[i]:
            signal(near_sem.at[i], peer)

    def hear(i):
        pl.semaphore_wait(near_sem.at[i], len(rounds[i]))

    load_freq.wait()
    tables = [
        expanded_table(freq_ref, q * times + i * size, NF * pair, size * RHS, 0).astype(BF16) for i in range(chunks)
    ]
    part = jnp.zeros((NF * pair, columns), F32)
    for i in range(chunks):
        load_dirs[i].wait()
        steps = dirs[i * size : (i + 1) * size].astype(F32).reshape(size * RHS, columns).astype(BF16)
        part = part + jnp.dot(tables[i], steps, preferred_element_type=F32)
    for load in (load_mask, load_noise, load_green, load_prior):
        load.start()
    for g in range(n_freq):
        piece = part[g * rows : (g + 1) * rows]
        spec_own[g] = piece
        spec_send[g] = piece.astype(BF16)

    pl.semaphore_wait(barrier, len(peers))
    spec_copies = []
    for off in (2, 3, 1) if n_freq == 4 else range(1, n_freq):
        copy = remote(
            spec_send.at[(q + off) % n_freq], spec_recv.at[off - 1], spec_ssem.at[off - 1], spec_rsem.at[off - 1],
            freq_peer(off),
        )
        copy.start()
        spec_copies.append(copy)
    tell(0)

    load_mask.wait()
    sensor = lax.broadcasted_iota(jnp.int32, (padded, SBLK), 0)
    block = lax.broadcasted_iota(jnp.int32, (padded, SBLK), 1)
    per = SENSORS // SBLK
    picks = jnp.where((sensor >= block * per) & (sensor < (block + 1) * per), 1.0, 0.0).astype(BF16)
    block8 = lax.broadcasted_iota(jnp.int32, (SBLK, LANES), 0)
    parts = []
    for b in range(columns // PBLK):
        value = jnp.zeros((SBLK, LANES), F32)
        for s in range(SBLK):
            value = jnp.where(block8 == s, mask_ref[b, s].astype(F32), value)
        parts.append(value)
    blocks = jnp.concatenate(parts, axis=1).astype(BF16)
    mask[...] = jnp.dot(picks, blocks, preferred_element_type=F32).astype(BF16)
    load_green.wait()
    for w in range(own_w):
        for c in range(2):
            kern[w, c, :SENSORS, :] = green[w, c] * mask[:SENSORS, :]
            kern[w, c, SENSORS:, :] = jnp.zeros((padded - SENSORS, columns), BF16)
    hear(0)
    tell(1)
    for w in range(own_w):
        for c in range(2):
            turned[w, c] = kern[w, c].T
    load_noise.wait()
    noise[...] = jnp.zeros_like(noise)
    for u in range(units):
        w, j = u // tiles, u % tiles
        width = min(LANES, SENSORS - j * LANES)
        row, half = place(u)
        noise[row, half, :, :width] = jnp.broadcast_to(
            noise_ref[w : w + 1, j * LANES : j * LANES + width], (pair, width)
        )
    hear(1)
    tell(2)

    total = spec_own[q]
    for off, copy in zip((2, 3, 1) if n_freq == 4 else range(1, n_freq), spec_copies):
        copy.wait_recv()
        total = total + spec_recv[off - 1].astype(F32)

    for w in range(own_w):
        first = total[w * pair : (w + 1) * pair]
        second = jnp.concatenate([-first[RHS:], first[:RHS]], axis=0)
        data = jnp.dot(first.astype(BF16), turned[w, 0], preferred_element_type=F32) + jnp.dot(
            second.astype(BF16), turned[w, 1], preferred_element_type=F32
        )
        data = data.astype(BF16)
        for j in range(tiles):
            row, half = place(w * tiles + j)
            data_send[row, half] = data[:, j * LANES : (j + 1) * LANES]

    def data_copy(off, count):
        to, here = (k + off) % PLANE, pl.ds(0, count)
        return remote(
            data_send.at[to, here], data_recv.at[off, here], data_ssem.at[off], data_rsem.at[off], plane_peer(to)
        )

    def sum_copy(off, count):
        here = pl.ds(0, count)
        return remote(sum_send.at[here], sum_recv.at[off, here], sum_ssem.at[off], sum_rsem.at[off], ring_peer(off))

    def weighted_copy(off, count):
        own = weighted.at[k, pl.ds(0, count)]
        return remote(own, own, w_ssem.at[off], w_rsem.at[k], plane_peer((k + off) % PLANE))

    def weighted_arrival(owner, count):
        own = weighted.at[owner, pl.ds(0, count)]
        return remote(own, own, w_ssem.at[0], w_rsem.at[owner], plane_peer((k + 1) % PLANE))

    far_plane = [off for off in (6, 2, 5, 7, 3, 1, 4)]
    far_ring = sorted(range(1, ring), key=lambda off: -min(off, ring - off))

    for off in far_plane:
        two = (k + off) % PLANE // extra == core
        pl.when(two)(data_copy(off, 2).start)
        pl.when(jnp.logical_not(two))(data_copy(off, 1).start)

    for i in range(chunks):
        first_time = q * times + i * size
        back[i] = (2.0 * expanded_table(freq_ref, first_time, size * RHS, NF * pair, 1)).astype(BF16)
    load_prior.wait()
    for i in range(chunks):
        steps = dirs[i * size : (i + 1) * size].astype(F32).reshape(size * RHS, columns)
        damped[i] = steps * prior_ref[...]

    def reduce(count):
        acc = data_send[k, :count].astype(F32)
        for off in reversed(far_plane):
            data_copy(off, count).wait_recv()
            acc = acc + data_recv[off, :count].astype(F32)
        sum_send[:count] = acc.astype(BF16)
        hear(2)
        for off in far_ring:
            sum_copy(off, count).start()
        for off in reversed(far_ring):
            sum_copy(off, count).wait_recv()
            acc = acc + sum_recv[off, :count].astype(F32)
        weighted[k, :count] = (acc * noise[k, :count]).astype(BF16)
        for off in far_plane:
            weighted_copy(off, count).start()

    def finish(count):
        for off in far_ring:
            sum_copy(off, count).wait_send()
        for off in far_plane:
            weighted_copy(off, count).wait_send()

    pl.when(has_extra)(functools.partial(reduce, 2))
    pl.when(jnp.logical_not(has_extra))(functools.partial(reduce, 1))

    for owner in range(PLANE):
        two = owner // extra == core
        other = k != owner
        pl.when(jnp.logical_and(other, two))(weighted_arrival(owner, 2).wait_recv)
        pl.when(jnp.logical_and(other, jnp.logical_not(two)))(weighted_arrival(owner, 1).wait_recv)

    image_copies = []
    for w in range(own_w):
        here = slice(w * pair, (w + 1) * pair)
        first = jnp.concatenate([weighted[place(w * tiles + j)] for j in range(tiles)], axis=1)
        wide = first.astype(F32)
        second = jnp.concatenate([wide[RHS:], -wide[:RHS]], axis=0).astype(BF16)
        image = jnp.dot(first, kern[w, 0], preferred_element_type=F32) + jnp.dot(
            second, kern[w, 1], preferred_element_type=F32
        )
        image = image.astype(BF16)
        image_send[w] = image
        images[q, w] = image
        for off in (2, 3, 1) if n_freq == 4 else range(1, n_freq):
            copy = remote(
                image_send.at[w], images.at[q, w], im_ssem.at[w, off - 1], im_rsem.at[w, off - 1], freq_peer(off)
            )
            copy.start()
            image_copies.append(copy)

    for copy in spec_copies:
        copy.wait_send()
    for off in far_plane:
        two = (k + off) % PLANE // extra == core
        pl.when(two)(data_copy(off, 2).wait_send)
        pl.when(jnp.logical_not(two))(data_copy(off, 1).wait_send)
    pl.when(has_extra)(functools.partial(finish, 2))
    pl.when(jnp.logical_not(has_extra))(functools.partial(finish, 1))
    for copy in image_copies:
        copy.wait_recv()
    every = images[...].reshape(NF * pair, columns)
    for i in range(chunks):
        summed = jnp.dot(back[i], every, preferred_element_type=F32)
        out_ref[i * size : (i + 1) * size] = (summed + damped[i]).reshape(size, RHS, columns).astype(BF16)
    for copy in image_copies:
        copy.wait_send()


def on_device(ring, n_freq, direction, green_blocks, block_mask, noise_weights, prior_precision, freq_index):
    times, _, columns = direction.shape
    own_w = NF // n_freq
    pair = 2 * RHS
    rows = own_w * pair
    keys = NF * pair
    tiles = -(-SENSORS // LANES)
    padded = tiles * LANES
    vmem = pltpu.VMEM
    dma = pltpu.SemaphoreType.DMA
    chunks = 3
    size = times // chunks
    operands = (
        direction, green_blocks, block_mask.T, noise_weights, freq_index, prior_precision.reshape(1, columns)
    )
    return pl.pallas_call(
        functools.partial(forward_kernel, ring, n_freq),
        out_shape=vmem(direction.shape, BF16),
        in_specs=[pl.BlockSpec(memory_space=pltpu.HBM)] * len(operands),
        out_specs=pl.BlockSpec(memory_space=vmem),
        scratch_shapes=[
            vmem((times, RHS, columns), BF16),
            vmem((own_w, 2, SENSORS, columns), BF16),
            pltpu.SMEM(block_mask.shape[::-1], jnp.int32),
            vmem((own_w, SENSORS), F32),
            pltpu.SMEM((NF,), jnp.int32),
            vmem((1, columns), F32),
            vmem((own_w, 2, padded, columns), BF16),
            vmem((own_w, 2, columns, padded), BF16),
            vmem((padded, columns), BF16),
            vmem((PLANE, 2, pair, LANES), F32),
            vmem((n_freq, rows, columns), F32),
            vmem((n_freq, rows, columns), BF16),
            vmem((n_freq - 1, rows, columns), BF16),
            vmem((PLANE, 2, pair, LANES), BF16),
            vmem((PLANE, 2, pair, LANES), BF16),
            vmem((2, pair, LANES), BF16),
            vmem((ring, 2, pair, LANES), BF16),
            vmem((PLANE, 2, pair, LANES), BF16),
            vmem((own_w, pair, columns), BF16),
            vmem((n_freq, own_w, pair, columns), BF16),
            vmem((chunks, size * RHS, keys), BF16),
            vmem((chunks, size * RHS, columns), F32),
            dma((5,)),
            dma((chunks,)),
            pltpu.SemaphoreType.REGULAR((3,)),
            dma((n_freq - 1,)),
            dma((n_freq - 1,)),
            dma((PLANE,)),
            dma((PLANE,)),
            dma((ring,)),
            dma((ring,)),
            dma((PLANE,)),
            dma((PLANE,)),
            dma((own_w, n_freq - 1)),
            dma((own_w, n_freq - 1)),
        ],
        compiler_params=pltpu.CompilerParams(
            collective_id=0, has_side_effects=True, vmem_limit_bytes=40 * 1024 * 1024
        ),
        name="forward",
    )(*(pltpu.with_memory_space_constraint(operand, pltpu.HBM) for operand in operands))


def solution(mesh):
    n_freq = mesh.shape["freq"]
    ring = mesh.shape["param"] // PLANE
    placed = (
        P("freq", None, "param"),
        P("freq", None, None, "param"),
        P(None, "param"),
        P("freq", None),
        P("param"),
        P(),
    )
    return jax.shard_map(
        functools.partial(on_device, ring, n_freq),
        mesh=mesh,
        in_specs=placed,
        out_specs=P("freq", None, "param"),
        check_vma=False,
    )
```

```python
import functools
import math

import jax
import jax.numpy as jnp
from jax import lax
from jax.experimental import pallas as pl
from jax.experimental.pallas import tpu as pltpu
from jax.sharding import PartitionSpec as P

NT = 420
NF = 8
RHS = 8
SENSORS = 600
SBLK = 8
PBLK = 128
LANES = 128
PLANE = 8
ROW = 4
MESH = pl.DeviceIdType.MESH
F32 = jnp.float32
BF16 = jnp.bfloat16


def trig(freq, component, time):
    turn = freq * time + component * (NT // 4)
    phase = turn - NT * jnp.floor(turn * (1.0 / NT))
    phase = jnp.where(phase < 0, phase + NT, phase)
    phase = jnp.where(phase >= NT, phase - NT, phase)
    y = (jnp.abs(phase - NT // 2) - NT // 4) * (2.0 * math.pi / NT)
    s = y * y
    poly = -1.0 / 39916800
    for coef in (1.0 / 362880, -1.0 / 5040, 1.0 / 120, -1.0 / 6, 1.0):
        poly = poly * s + coef
    return poly * y * (1.0 / math.sqrt(NT))


def expanded_table(freq_ref, first_time, rows, columns, key_axis):
    key_shape = (rows, 1) if key_axis == 0 else (1, columns)
    step_shape = (1, columns) if key_axis == 0 else (rows, 1)
    key = lax.broadcasted_iota(jnp.int32, key_shape, key_axis)
    step = lax.broadcasted_iota(jnp.int32, step_shape, 1 - key_axis)
    freq = jnp.zeros(key_shape, F32)
    for w in range(NF):
        freq = jnp.where(key // (2 * RHS) == w, freq_ref[w].astype(F32), freq)
    component = (key // RHS % 2).astype(F32)
    time = (step // RHS + first_time).astype(F32)
    values = trig(freq, component, time)
    return jnp.where(key % RHS == step % RHS, values, 0.0)


def forward_kernel(
    ring, n_freq, dir_hbm, green_hbm, mask_hbm, noise_hbm, freq_hbm, prior_hbm,
    out_ref,
    dirs, green, mask_ref, noise_ref, freq_ref, prior_ref, kern, turned, mask, noise,
    spec_own, spec_send, spec_recv, data_send, data_recv, sum_send, sum_recv, weighted, image_send, images, back, damped,
    load_sem, dir_sem, near_sem,
    spec_ssem, spec_rsem, data_ssem, data_rsem, sum_ssem, sum_rsem, w_ssem, w_rsem, im_ssem, im_rsem,
):
    param = lax.axis_index("param")
    q = lax.axis_index("freq")
    k, z = param // ring, param % ring
    core = q % 2
    times = dirs.shape[0]
    columns = dirs.shape[2]
    own_w = NF // n_freq
    pair = 2 * RHS
    rows = own_w * pair
    tiles = -(-SENSORS // LANES)
    units = own_w * tiles
    padded = tiles * LANES
    extra = 2 * (units - PLANE)
    has_extra = k // extra == core

    def place(u, half):
        return (u, half) if u < PLANE else (extra * core + 2 * (u - PLANE) + half, 2)

    def freq_peer(off):
        return (param, (q + off) % n_freq)

    def plane_peer(to):
        return (to * ring + z, q)

    def ring_peer(off):
        return (k * ring + (z + off) % ring, q)

    def remote(src, dst, ssem, rsem, to):
        return pltpu.make_async_remote_copy(
            src_ref=src, dst_ref=dst, send_sem=ssem, recv_sem=rsem, device_id=to, device_id_type=MESH
        )

    def signal(semaphore, to):
        pl.semaphore_signal(semaphore, inc=1, device_id=to, device_id_type=MESH)

    load_freq, load_mask, load_noise, load_prior, load_green = [
        pltpu.make_async_copy(src, dst, load_sem.at[i])
        for i, (src, dst) in enumerate(
            (
                (freq_hbm, freq_ref), (mask_hbm, mask_ref), (noise_hbm, noise_ref), (prior_hbm, prior_ref),
                (green_hbm, green),
            )
        )
    ]
    chunks = dir_sem.shape[0]
    size = times // chunks
    load_dirs = [
        pltpu.make_async_copy(dir_hbm.at[pl.ds(i * size, size)], dirs.at[pl.ds(i * size, size)], dir_sem.at[i])
        for i in range(chunks)
    ]
    for load in [load_freq] + load_dirs:
        load.start()

    y, x = k // ROW, k % ROW
    beside = [plane_peer(y * ROW + (x + 1) % ROW), plane_peer(y * ROW + (x + ROW - 1) % ROW)]
    across = [plane_peer((y + 1) % (PLANE // ROW) * ROW + x)]

    def along(d):
        return [ring_peer(d), ring_peer(ring - d)]

    barrier = pltpu.get_barrier_semaphore()
    peers = [freq_peer(o) for o in range(1, n_freq)] + beside + across + along(1)
    for peer in peers:
        signal(barrier, peer)
    rounds = [beside + across + along(1), beside + along(2), along(4)]

    def tell(i):
        for peer in rounds[i]:
            signal(near_sem.at[i], peer)

    def hear(i):
        pl.semaphore_wait(near_sem.at[i], len(rounds[i]))

    key = lax.broadcasted_iota(jnp.int32, (NF * pair, 1), 0)
    step = lax.broadcasted_iota(jnp.int32, (1, LANES), 1)
    row = lax.broadcasted_iota(jnp.int32, (NF * pair, size * RHS), 0)
    column = lax.broadcasted_iota(jnp.int32, (NF * pair, size * RHS), 1)
    same_side = row % RHS == column % RHS
    repeats = [jnp.where(row == column // RHS + i * size, 1.0, 0.0).astype(BF16) for i in range(chunks)]
    load_freq.wait()
    freq = jnp.zeros(key.shape, F32)
    for w in range(NF):
        freq = jnp.where(key // pair == w, freq_ref[w].astype(F32), freq)
    narrow = trig(freq, (key // RHS % 2).astype(F32), (step + q * times).astype(F32)).astype(BF16)
    tables = [
        jnp.where(same_side, jnp.dot(narrow, repeat, preferred_element_type=F32), 0.0).astype(BF16)
        for repeat in repeats
    ]
    part = jnp.zeros((NF * pair, columns), F32)
    for i in range(chunks):
        load_dirs[i].wait()
        steps = dirs[i * size : (i + 1) * size].astype(F32).reshape(size * RHS, columns).astype(BF16)
        part = part + jnp.dot(tables[i], steps, preferred_element_type=F32)
    for load in (load_mask, load_noise, load_green, load_prior):
        load.start()
    for g in range(n_freq):
        piece = part[g * rows : (g + 1) * rows]
        spec_own[g] = piece
        spec_send[g] = piece.astype(BF16)

    pl.semaphore_wait(barrier, len(peers))
    spec_copies = []
    for off in (2, 3, 1) if n_freq == 4 else range(1, n_freq):
        copy = remote(
            spec_send.at[(q + off) % n_freq], spec_recv.at[off - 1], spec_ssem.at[off - 1], spec_rsem.at[off - 1],
            freq_peer(off),
        )
        copy.start()
        spec_copies.append(copy)
    tell(0)

    load_mask.wait()
    sensor = lax.broadcasted_iota(jnp.int32, (padded, SBLK), 0)
    block = lax.broadcasted_iota(jnp.int32, (padded, SBLK), 1)
    per = SENSORS // SBLK
    picks = jnp.where((sensor >= block * per) & (sensor < (block + 1) * per), 1.0, 0.0).astype(BF16)
    block8 = lax.broadcasted_iota(jnp.int32, (SBLK, LANES), 0)
    parts = []
    for b in range(columns // PBLK):
        value = jnp.zeros((SBLK, LANES), F32)
        for s in range(SBLK):
            value = jnp.where(block8 == s, mask_ref[b, s].astype(F32), value)
        parts.append(value)
    blocks = jnp.concatenate(parts, axis=1).astype(BF16)
    mask[...] = jnp.dot(picks, blocks, preferred_element_type=F32).astype(BF16)
    load_green.wait()
    for w in range(own_w):
        for c in range(2):
            kern[w, c, :SENSORS, :] = green[w, c] * mask[:SENSORS, :]
            kern[w, c, SENSORS:, :] = jnp.zeros((padded - SENSORS, columns), BF16)
    hear(0)
    tell(1)
    for w in range(own_w):
        for c in range(2):
            turned[w, c] = kern[w, c].T
    load_noise.wait()
    noise[...] = jnp.zeros_like(noise)
    for u in range(units):
        w, j = u // tiles, u % tiles
        width = min(LANES, SENSORS - j * LANES)
        for half in range(2):
            row, part = place(u, half)
            noise[row, part, :, :width] = jnp.broadcast_to(
                noise_ref[w : w + 1, j * LANES : j * LANES + width], (RHS, width)
            )
    hear(1)
    tell(2)

    total = spec_own[q]
    for off, copy in zip((2, 3, 1) if n_freq == 4 else range(1, n_freq), spec_copies):
        copy.wait_recv()
        total = total + spec_recv[off - 1].astype(F32)

    for w in range(own_w):
        first = total[w * pair : (w + 1) * pair]
        second = jnp.concatenate([-first[RHS:], first[:RHS]], axis=0)
        data = jnp.dot(first.astype(BF16), turned[w, 0], preferred_element_type=F32) + jnp.dot(
            second.astype(BF16), turned[w, 1], preferred_element_type=F32
        )
        for j in range(tiles):
            for half in range(2):
                row, part = place(w * tiles + j, half)
                data_send[row, part] = data[half * RHS : (half + 1) * RHS, j * LANES : (j + 1) * LANES].astype(BF16)

    def data_copy(off, count):
        to, here = (k + off) % PLANE, pl.ds(0, count)
        return remote(
            data_send.at[to, here], data_recv.at[off, here], data_ssem.at[off], data_rsem.at[off], plane_peer(to)
        )

    def sum_copy(off, count):
        here = pl.ds(0, count)
        return remote(sum_send.at[here], sum_recv.at[off, here], sum_ssem.at[off], sum_rsem.at[off], ring_peer(off))

    def weighted_copy(off, count):
        own = weighted.at[k, pl.ds(0, count)]
        return remote(own, own, w_ssem.at[off], w_rsem.at[k], plane_peer((k + off) % PLANE))

    def weighted_arrival(owner, count):
        own = weighted.at[owner, pl.ds(0, count)]
        return remote(own, own, w_ssem.at[0], w_rsem.at[owner], plane_peer((k + 1) % PLANE))

    far_plane = [off for off in (6, 2, 5, 7, 3, 1, 4)]
    far_ring = sorted(range(1, ring), key=lambda off: -min(off, ring - off))

    for off in far_plane:
        two = (k + off) % PLANE // extra == core
        pl.when(two)(data_copy(off, 3).start)
        pl.when(jnp.logical_not(two))(data_copy(off, 2).start)

    for i in range(chunks):
        first_time = q * times + i * size
        back[i] = (2.0 * expanded_table(freq_ref, first_time, size * RHS, NF * pair, 1)).astype(BF16)
    load_prior.wait()
    for i in range(chunks):
        steps = dirs[i * size : (i + 1) * size].astype(F32).reshape(size * RHS, columns)
        damped[i] = steps * prior_ref[...]

    def reduce(count):
        acc = data_send[k, :count].astype(F32)
        for off in reversed(far_plane):
            data_copy(off, count).wait_recv()
            acc = acc + data_recv[off, :count].astype(F32)
        sum_send[:count] = acc.astype(BF16)
        hear(2)
        for off in far_ring:
            sum_copy(off, count).start()
        for off in reversed(far_ring):
            sum_copy(off, count).wait_recv()
            acc = acc + sum_recv[off, :count].astype(F32)
        weighted[k, :count] = (acc * noise[k, :count]).astype(BF16)
        for off in far_plane:
            weighted_copy(off, count).start()

    def finish(count):
        for off in far_ring:
            sum_copy(off, count).wait_send()
        for off in far_plane:
            weighted_copy(off, count).wait_send()

    pl.when(has_extra)(functools.partial(reduce, 3))
    pl.when(jnp.logical_not(has_extra))(functools.partial(reduce, 2))

    image_copies = []
    for w in range(own_w):
        for owner in range(PLANE) if w == 0 else ():
            two = owner // extra == core
            other = k != owner
            pl.when(jnp.logical_and(other, two))(weighted_arrival(owner, 3).wait_recv)
            pl.when(jnp.logical_and(other, jnp.logical_not(two)))(weighted_arrival(owner, 2).wait_recv)
        halves = [
            jnp.concatenate([weighted[place(w * tiles + j, half)].astype(F32) for j in range(tiles)], axis=1)
            for half in range(2)
        ]
        wide = jnp.concatenate(halves, axis=0)
        first = wide.astype(BF16)
        second = jnp.concatenate([halves[1], -halves[0]], axis=0).astype(BF16)
        image = jnp.dot(first, kern[w, 0], preferred_element_type=F32) + jnp.dot(
            second, kern[w, 1], preferred_element_type=F32
        )
        image = image.astype(BF16)
        image_send[w] = image
        images[q, w] = image
        for off in (2, 3, 1) if n_freq == 4 else range(1, n_freq):
            copy = remote(
                image_send.at[w], images.at[q, w], im_ssem.at[w, off - 1], im_rsem.at[w, off - 1], freq_peer(off)
            )
            copy.start()
            image_copies.append(copy)

    for copy in spec_copies:
        copy.wait_send()
    for off in far_plane:
        two = (k + off) % PLANE // extra == core
        pl.when(two)(data_copy(off, 3).wait_send)
        pl.when(jnp.logical_not(two))(data_copy(off, 2).wait_send)
    pl.when(has_extra)(functools.partial(finish, 3))
    pl.when(jnp.logical_not(has_extra))(functools.partial(finish, 2))
    for copy in image_copies:
        copy.wait_recv()
    every = images[...].reshape(NF * pair, columns)
    for i in range(chunks):
        summed = jnp.dot(back[i], every, preferred_element_type=F32)
        out_ref[i * size : (i + 1) * size] = (summed + damped[i]).reshape(size, RHS, columns).astype(BF16)
    for copy in image_copies:
        copy.wait_send()


def on_device(ring, n_freq, direction, green_blocks, block_mask, noise_weights, prior_precision, freq_index):
    times, _, columns = direction.shape
    own_w = NF // n_freq
    pair = 2 * RHS
    rows = own_w * pair
    keys = NF * pair
    tiles = -(-SENSORS // LANES)
    padded = tiles * LANES
    vmem = pltpu.VMEM
    dma = pltpu.SemaphoreType.DMA
    chunks = 3
    size = times // chunks
    operands = (
        direction, green_blocks, block_mask.T, noise_weights, freq_index, prior_precision.reshape(1, columns)
    )
    return pl.pallas_call(
        functools.partial(forward_kernel, ring, n_freq),
        out_shape=vmem(direction.shape, BF16),
        in_specs=[pl.BlockSpec(memory_space=pltpu.HBM)] * len(operands),
        out_specs=pl.BlockSpec(memory_space=vmem),
        scratch_shapes=[
            vmem((times, RHS, columns), BF16),
            vmem((own_w, 2, SENSORS, columns), BF16),
            pltpu.SMEM(block_mask.shape[::-1], jnp.int32),
            vmem((own_w, SENSORS), F32),
            pltpu.SMEM((NF,), jnp.int32),
            vmem((1, columns), F32),
            vmem((own_w, 2, padded, columns), BF16),
            vmem((own_w, 2, columns, padded), BF16),
            vmem((padded, columns), BF16),
            vmem((PLANE, 3, RHS, LANES), F32),
            vmem((n_freq, rows, columns), F32),
            vmem((n_freq, rows, columns), BF16),
            vmem((n_freq - 1, rows, columns), BF16),
            vmem((PLANE, 3, RHS, LANES), BF16),
            vmem((PLANE, 3, RHS, LANES), BF16),
            vmem((3, RHS, LANES), BF16),
            vmem((ring, 3, RHS, LANES), BF16),
            vmem((PLANE, 3, RHS, LANES), BF16),
            vmem((own_w, pair, columns), BF16),
            vmem((n_freq, own_w, pair, columns), BF16),
            vmem((chunks, size * RHS, keys), BF16),
            vmem((chunks, size * RHS, columns), F32),
            dma((5,)),
            dma((chunks,)),
            pltpu.SemaphoreType.REGULAR((3,)),
            dma((n_freq - 1,)),
            dma((n_freq - 1,)),
            dma((PLANE,)),
            dma((PLANE,)),
            dma((ring,)),
            dma((ring,)),
            dma((PLANE,)),
            dma((PLANE,)),
            dma((own_w, n_freq - 1)),
            dma((own_w, n_freq - 1)),
        ],
        compiler_params=pltpu.CompilerParams(
            collective_id=0, has_side_effects=True, vmem_limit_bytes=40 * 1024 * 1024
        ),
        name="forward",
    )(*(pltpu.with_memory_space_constraint(operand, pltpu.HBM) for operand in operands))


def solution(mesh):
    n_freq = mesh.shape["freq"]
    ring = mesh.shape["param"] // PLANE
    placed = (
        P("freq", None, "param"),
        P("freq", None, None, "param"),
        P(None, "param"),
        P("freq", None),
        P("param"),
        P(),
    )
    return jax.shard_map(
        functools.partial(on_device, ring, n_freq),
        mesh=mesh,
        in_specs=placed,
        out_specs=P("freq", None, "param"),
        check_vma=False,
    )
```

```python
import functools
import math

import jax
import jax.numpy as jnp
from jax import lax
from jax.experimental import pallas as pl
from jax.experimental.pallas import tpu as pltpu
from jax.sharding import PartitionSpec as P

NT = 420
NF = 8
RHS = 8
SENSORS = 600
SBLK = 8
PBLK = 128
LANES = 128
PLANE = 8
ROW = 4
MESH = pl.DeviceIdType.MESH
F32 = jnp.float32
BF16 = jnp.bfloat16


def trig(freq, component, time):
    turn = freq * time + component * (NT // 4)
    phase = turn - NT * jnp.floor(turn * (1.0 / NT))
    phase = jnp.where(phase < 0, phase + NT, phase)
    phase = jnp.where(phase >= NT, phase - NT, phase)
    y = (jnp.abs(phase - NT // 2) - NT // 4) * (2.0 * math.pi / NT)
    s = y * y
    poly = -1.0 / 39916800
    for coef in (1.0 / 362880, -1.0 / 5040, 1.0 / 120, -1.0 / 6, 1.0):
        poly = poly * s + coef
    return poly * y * (1.0 / math.sqrt(NT))


def expanded_table(freq_ref, first_time, rows, columns, key_axis):
    key_shape = (rows, 1) if key_axis == 0 else (1, columns)
    step_shape = (1, columns) if key_axis == 0 else (rows, 1)
    key = lax.broadcasted_iota(jnp.int32, key_shape, key_axis)
    step = lax.broadcasted_iota(jnp.int32, step_shape, 1 - key_axis)
    freq = jnp.zeros(key_shape, F32)
    for w in range(NF):
        freq = jnp.where(key // (2 * RHS) == w, freq_ref[w].astype(F32), freq)
    component = (key // RHS % 2).astype(F32)
    time = (step // RHS + first_time).astype(F32)
    values = trig(freq, component, time)
    return jnp.where(key % RHS == step % RHS, values, 0.0)


def forward_kernel(
    ring, n_freq, dir_hbm, green_hbm, mask_hbm, noise_hbm, freq_hbm, prior_hbm,
    out_ref,
    dirs, green, mask_ref, noise_ref, freq_ref, prior_ref, kern, turned, mask, noise,
    spec_own, spec_send, spec_recv, data_send, data_recv, sum_send, sum_recv, weighted, image_send, images, back, damped,
    load_sem, dir_sem, near_sem,
    spec_ssem, spec_rsem, data_ssem, data_rsem, sum_ssem, sum_rsem, w_ssem, w_rsem, im_ssem, im_rsem,
):
    param = lax.axis_index("param")
    q = lax.axis_index("freq")
    k, z = param // ring, param % ring
    core = q % 2
    times = dirs.shape[0]
    columns = dirs.shape[2]
    own_w = NF // n_freq
    pair = 2 * RHS
    rows = own_w * pair
    tiles = -(-SENSORS // LANES)
    units = own_w * tiles
    padded = tiles * LANES
    extra = 2 * (units - PLANE)
    has_extra = k // extra == core

    def place(u, half):
        return (u, half) if u < PLANE else (extra * core + 2 * (u - PLANE) + half, 2)

    def freq_peer(off):
        return (param, (q + off) % n_freq)

    def plane_peer(to):
        return (to * ring + z, q)

    def ring_peer(off):
        return (k * ring + (z + off) % ring, q)

    def remote(src, dst, ssem, rsem, to):
        return pltpu.make_async_remote_copy(
            src_ref=src, dst_ref=dst, send_sem=ssem, recv_sem=rsem, device_id=to, device_id_type=MESH
        )

    def signal(semaphore, to):
        pl.semaphore_signal(semaphore, inc=1, device_id=to, device_id_type=MESH)

    load_freq, load_mask, load_noise, load_prior, load_green = [
        pltpu.make_async_copy(src, dst, load_sem.at[i])
        for i, (src, dst) in enumerate(
            (
                (freq_hbm, freq_ref), (mask_hbm, mask_ref), (noise_hbm, noise_ref), (prior_hbm, prior_ref),
                (green_hbm, green),
            )
        )
    ]
    chunks = dir_sem.shape[0]
    size = times // chunks
    load_dirs = [
        pltpu.make_async_copy(dir_hbm.at[pl.ds(i * size, size)], dirs.at[pl.ds(i * size, size)], dir_sem.at[i])
        for i in range(chunks)
    ]
    for load in [load_freq] + load_dirs:
        load.start()

    y, x = k // ROW, k % ROW
    beside = [plane_peer(y * ROW + (x + 1) % ROW), plane_peer(y * ROW + (x + ROW - 1) % ROW)]
    across = [plane_peer((y + 1) % (PLANE // ROW) * ROW + x)]

    def along(d):
        return [ring_peer(d), ring_peer(ring - d)]

    barrier = pltpu.get_barrier_semaphore()
    peers = [freq_peer(o) for o in range(1, n_freq)] + beside + across + along(1)
    for peer in peers:
        signal(barrier, peer)
    rounds = [beside + across + along(1), beside + along(2), along(4)]

    def tell(i):
        for peer in rounds[i]:
            signal(near_sem.at[i], peer)

    def hear(i):
        pl.semaphore_wait(near_sem.at[i], len(rounds[i]))

    key = lax.broadcasted_iota(jnp.int32, (NF * pair, 1), 0)
    step = lax.broadcasted_iota(jnp.int32, (1, LANES), 1)
    row = lax.broadcasted_iota(jnp.int32, (NF * pair, size * RHS), 0)
    column = lax.broadcasted_iota(jnp.int32, (NF * pair, size * RHS), 1)
    same_side = row % RHS == column % RHS
    repeats = [jnp.where(row == column // RHS + i * size, 1.0, 0.0).astype(BF16) for i in range(chunks)]
    load_freq.wait()
    freq = jnp.zeros(key.shape, F32)
    for w in range(NF):
        freq = jnp.where(key // pair == w, freq_ref[w].astype(F32), freq)
    narrow = trig(freq, (key // RHS % 2).astype(F32), (step + q * times).astype(F32)).astype(BF16)
    tables = [
        jnp.where(same_side, jnp.dot(narrow, repeat, preferred_element_type=F32), 0.0).astype(BF16)
        for repeat in repeats
    ]
    part = jnp.zeros((NF * pair, columns), F32)
    for i in range(chunks):
        load_dirs[i].wait()
        steps = dirs[i * size : (i + 1) * size].astype(F32).reshape(size * RHS, columns).astype(BF16)
        part = part + jnp.dot(tables[i], steps, preferred_element_type=F32)
    for load in (load_mask, load_noise, load_green, load_prior):
        load.start()
    for g in range(n_freq):
        piece = part[g * rows : (g + 1) * rows]
        spec_send[g] = piece.astype(BF16)

    pl.semaphore_wait(barrier, len(peers))
    spec_copies = []
    for off in (2, 3, 1) if n_freq == 4 else range(1, n_freq):
        copy = remote(
            spec_send.at[(q + off) % n_freq], spec_recv.at[off - 1], spec_ssem.at[off - 1], spec_rsem.at[off - 1],
            freq_peer(off),
        )
        copy.start()
        spec_copies.append(copy)
    tell(0)
    for g in range(n_freq):
        spec_own[g] = part[g * rows : (g + 1) * rows]

    load_mask.wait()
    sensor = lax.broadcasted_iota(jnp.int32, (padded, SBLK), 0)
    block = lax.broadcasted_iota(jnp.int32, (padded, SBLK), 1)
    per = SENSORS // SBLK
    picks = jnp.where((sensor >= block * per) & (sensor < (block + 1) * per), 1.0, 0.0).astype(BF16)
    block8 = lax.broadcasted_iota(jnp.int32, (SBLK, LANES), 0)
    parts = []
    for b in range(columns // PBLK):
        value = jnp.zeros((SBLK, LANES), F32)
        for s in range(SBLK):
            value = jnp.where(block8 == s, mask_ref[b, s].astype(F32), value)
        parts.append(value)
    blocks = jnp.concatenate(parts, axis=1).astype(BF16)
    mask[...] = jnp.dot(picks, blocks, preferred_element_type=F32).astype(BF16)
    hear(0)
    tell(1)
    load_green.wait()
    for w in range(own_w):
        for c in range(2):
            kern[w, c, :SENSORS, :] = green[w, c] * mask[:SENSORS, :]
            kern[w, c, SENSORS:, :] = jnp.zeros((padded - SENSORS, columns), BF16)
    for w in range(own_w):
        for c in range(2):
            turned[w, c] = kern[w, c].T
    load_noise.wait()
    noise[...] = jnp.zeros_like(noise)
    for u in range(units):
        w, j = u // tiles, u % tiles
        width = min(LANES, SENSORS - j * LANES)
        for half in range(2):
            row, part = place(u, half)
            noise[row, part, :, :width] = jnp.broadcast_to(
                noise_ref[w : w + 1, j * LANES : j * LANES + width], (RHS, width)
            )
    hear(1)
    tell(2)

    total = spec_own[q]
    for off, copy in zip((2, 3, 1) if n_freq == 4 else range(1, n_freq), spec_copies):
        copy.wait_recv()
        total = total + spec_recv[off - 1].astype(F32)

    for w in range(own_w):
        first = total[w * pair : (w + 1) * pair]
        second = jnp.concatenate([-first[RHS:], first[:RHS]], axis=0)
        data = jnp.dot(first.astype(BF16), turned[w, 0], preferred_element_type=F32) + jnp.dot(
            second.astype(BF16), turned[w, 1], preferred_element_type=F32
        )
        for j in range(tiles):
            for half in range(2):
                row, part = place(w * tiles + j, half)
                data_send[row, part] = data[half * RHS : (half + 1) * RHS, j * LANES : (j + 1) * LANES].astype(BF16)

    def data_copy(off, count):
        to, here = (k + off) % PLANE, pl.ds(0, count)
        return remote(
            data_send.at[to, here], data_recv.at[off, here], data_ssem.at[off], data_rsem.at[off], plane_peer(to)
        )

    def sum_copy(off, count):
        here = pl.ds(0, count)
        return remote(sum_send.at[here], sum_recv.at[off, here], sum_ssem.at[off], sum_rsem.at[off], ring_peer(off))

    def weighted_copy(off, count):
        own = weighted.at[k, pl.ds(0, count)]
        return remote(own, own, w_ssem.at[off], w_rsem.at[k], plane_peer((k + off) % PLANE))

    def weighted_arrival(owner, count):
        own = weighted.at[owner, pl.ds(0, count)]
        return remote(own, own, w_ssem.at[0], w_rsem.at[owner], plane_peer((k + 1) % PLANE))

    far_plane = [off for off in (6, 2, 5, 7, 3, 1, 4)]
    far_ring = sorted(range(1, ring), key=lambda off: -min(off, ring - off))

    for off in far_plane:
        two = (k + off) % PLANE // extra == core
        pl.when(two)(data_copy(off, 3).start)
        pl.when(jnp.logical_not(two))(data_copy(off, 2).start)

    for i in range(chunks):
        first_time = q * times + i * size
        back[i] = (2.0 * expanded_table(freq_ref, first_time, size * RHS, NF * pair, 1)).astype(BF16)
    load_prior.wait()
    for i in range(chunks):
        steps = dirs[i * size : (i + 1) * size].astype(F32).reshape(size * RHS, columns)
        damped[i] = steps * prior_ref[...]

    def reduce(count):
        acc = data_send[k, :count].astype(F32)
        for off in reversed(far_plane):
            data_copy(off, count).wait_recv()
            acc = acc + data_recv[off, :count].astype(F32)
        sum_send[:count] = acc.astype(BF16)
        hear(2)
        for off in far_ring:
            sum_copy(off, count).start()
        for off in reversed(far_ring):
            sum_copy(off, count).wait_recv()
            acc = acc + sum_recv[off, :count].astype(F32)
        weighted[k, :count] = (acc * noise[k, :count]).astype(BF16)
        for off in far_plane:
            weighted_copy(off, count).start()

    def finish(count):
        for off in far_ring:
            sum_copy(off, count).wait_send()
        for off in far_plane:
            weighted_copy(off, count).wait_send()

    pl.when(has_extra)(functools.partial(reduce, 3))
    pl.when(jnp.logical_not(has_extra))(functools.partial(reduce, 2))

    image_copies = []
    for w in range(own_w):
        for owner in range(PLANE) if w == 0 else ():
            two = owner // extra == core
            other = k != owner
            pl.when(jnp.logical_and(other, two))(weighted_arrival(owner, 3).wait_recv)
            pl.when(jnp.logical_and(other, jnp.logical_not(two)))(weighted_arrival(owner, 2).wait_recv)
        halves = [
            jnp.concatenate([weighted[place(w * tiles + j, half)].astype(F32) for j in range(tiles)], axis=1)
            for half in range(2)
        ]
        wide = jnp.concatenate(halves, axis=0)
        first = wide.astype(BF16)
        second = jnp.concatenate([halves[1], -halves[0]], axis=0).astype(BF16)
        image = jnp.dot(first, kern[w, 0], preferred_element_type=F32) + jnp.dot(
            second, kern[w, 1], preferred_element_type=F32
        )
        image = image.astype(BF16)
        image_send[w] = image
        images[q, w] = image
        for off in (2, 3, 1) if n_freq == 4 else range(1, n_freq):
            copy = remote(
                image_send.at[w], images.at[q, w], im_ssem.at[w, off - 1], im_rsem.at[w, off - 1], freq_peer(off)
            )
            copy.start()
            image_copies.append(copy)

    for copy in spec_copies:
        copy.wait_send()
    for off in far_plane:
        two = (k + off) % PLANE // extra == core
        pl.when(two)(data_copy(off, 3).wait_send)
        pl.when(jnp.logical_not(two))(data_copy(off, 2).wait_send)
    pl.when(has_extra)(functools.partial(finish, 3))
    pl.when(jnp.logical_not(has_extra))(functools.partial(finish, 2))
    for copy in image_copies:
        copy.wait_recv()
    every = images[...].reshape(NF * pair, columns)
    for i in range(chunks):
        summed = jnp.dot(back[i], every, preferred_element_type=F32)
        out_ref[i * size : (i + 1) * size] = (summed + damped[i]).reshape(size, RHS, columns).astype(BF16)
    for copy in image_copies:
        copy.wait_send()


def on_device(ring, n_freq, direction, green_blocks, block_mask, noise_weights, prior_precision, freq_index):
    times, _, columns = direction.shape
    own_w = NF // n_freq
    pair = 2 * RHS
    rows = own_w * pair
    keys = NF * pair
    tiles = -(-SENSORS // LANES)
    padded = tiles * LANES
    vmem = pltpu.VMEM
    dma = pltpu.SemaphoreType.DMA
    chunks = 3
    size = times // chunks
    operands = (
        direction, green_blocks, block_mask.T, noise_weights, freq_index, prior_precision.reshape(1, columns)
    )
    return pl.pallas_call(
        functools.partial(forward_kernel, ring, n_freq),
        out_shape=vmem(direction.shape, BF16),
        in_specs=[pl.BlockSpec(memory_space=pltpu.HBM)] * len(operands),
        out_specs=pl.BlockSpec(memory_space=vmem),
        scratch_shapes=[
            vmem((times, RHS, columns), BF16),
            vmem((own_w, 2, SENSORS, columns), BF16),
            pltpu.SMEM(block_mask.shape[::-1], jnp.int32),
            vmem((own_w, SENSORS), F32),
            pltpu.SMEM((NF,), jnp.int32),
            vmem((1, columns), F32),
            vmem((own_w, 2, padded, columns), BF16),
            vmem((own_w, 2, columns, padded), BF16),
            vmem((padded, columns), BF16),
            vmem((PLANE, 3, RHS, LANES), F32),
            vmem((n_freq, rows, columns), F32),
            vmem((n_freq, rows, columns), BF16),
            vmem((n_freq - 1, rows, columns), BF16),
            vmem((PLANE, 3, RHS, LANES), BF16),
            vmem((PLANE, 3, RHS, LANES), BF16),
            vmem((3, RHS, LANES), BF16),
            vmem((ring, 3, RHS, LANES), BF16),
            vmem((PLANE, 3, RHS, LANES), BF16),
            vmem((own_w, pair, columns), BF16),
            vmem((n_freq, own_w, pair, columns), BF16),
            vmem((chunks, size * RHS, keys), BF16),
            vmem((chunks, size * RHS, columns), F32),
            dma((5,)),
            dma((chunks,)),
            pltpu.SemaphoreType.REGULAR((3,)),
            dma((n_freq - 1,)),
            dma((n_freq - 1,)),
            dma((PLANE,)),
            dma((PLANE,)),
            dma((ring,)),
            dma((ring,)),
            dma((PLANE,)),
            dma((PLANE,)),
            dma((own_w, n_freq - 1)),
            dma((own_w, n_freq - 1)),
        ],
        compiler_params=pltpu.CompilerParams(
            collective_id=0, has_side_effects=True, vmem_limit_bytes=40 * 1024 * 1024
        ),
        name="forward",
    )(*(pltpu.with_memory_space_constraint(operand, pltpu.HBM) for operand in operands))


def solution(mesh):
    n_freq = mesh.shape["freq"]
    ring = mesh.shape["param"] // PLANE
    placed = (
        P("freq", None, "param"),
        P("freq", None, None, "param"),
        P(None, "param"),
        P("freq", None),
        P("param"),
        P(),
    )
    return jax.shard_map(
        functools.partial(on_device, ring, n_freq),
        mesh=mesh,
        in_specs=placed,
        out_specs=P("freq", None, "param"),
        check_vma=False,
    )
```

```python
import functools
import math

import jax
import jax.numpy as jnp
from jax import lax
from jax.experimental import pallas as pl
from jax.experimental.pallas import tpu as pltpu
from jax.sharding import PartitionSpec as P

NT = 420
NF = 8
RHS = 8
SENSORS = 600
SBLK = 8
PBLK = 128
LANES = 128
PLANE = 8
ROW = 4
MESH = pl.DeviceIdType.MESH
F32 = jnp.float32
BF16 = jnp.bfloat16


def trig(freq, component, time):
    turn = freq * time + component * (NT // 4)
    phase = turn - NT * jnp.floor(turn * (1.0 / NT))
    phase = jnp.where(phase < 0, phase + NT, phase)
    phase = jnp.where(phase >= NT, phase - NT, phase)
    y = (jnp.abs(phase - NT // 2) - NT // 4) * (2.0 * math.pi / NT)
    s = y * y
    poly = -1.0 / 39916800
    for coef in (1.0 / 362880, -1.0 / 5040, 1.0 / 120, -1.0 / 6, 1.0):
        poly = poly * s + coef
    return poly * y * (1.0 / math.sqrt(NT))


def expanded_table(freq_ref, first_time, rows, columns, key_axis):
    key_shape = (rows, 1) if key_axis == 0 else (1, columns)
    step_shape = (1, columns) if key_axis == 0 else (rows, 1)
    key = lax.broadcasted_iota(jnp.int32, key_shape, key_axis)
    step = lax.broadcasted_iota(jnp.int32, step_shape, 1 - key_axis)
    freq = jnp.zeros(key_shape, F32)
    for w in range(NF):
        freq = jnp.where(key // (2 * RHS) == w, freq_ref[w].astype(F32), freq)
    component = (key // RHS % 2).astype(F32)
    time = (step // RHS + first_time).astype(F32)
    values = trig(freq, component, time)
    return jnp.where(key % RHS == step % RHS, values, 0.0)


def forward_kernel(
    ring, n_freq, dir_hbm, green_hbm, mask_hbm, noise_hbm, freq_hbm, prior_hbm,
    out_ref,
    dirs, green, mask_ref, noise_ref, freq_ref, prior_ref, kern, turned, mask, noise,
    spec_own, spec_send, spec_recv, data_send, data_recv, sum_send, sum_recv, weighted, image_send, images, back, damped,
    load_sem, dir_sem, near_sem,
    spec_ssem, spec_rsem, data_ssem, data_rsem, sum_ssem, sum_rsem, w_ssem, w_rsem, im_ssem, im_rsem,
):
    param = lax.axis_index("param")
    q = lax.axis_index("freq")
    k, z = param // ring, param % ring
    core = q % 2
    times = dirs.shape[0]
    columns = dirs.shape[2]
    own_w = NF // n_freq
    pair = 2 * RHS
    rows = own_w * pair
    tiles = -(-SENSORS // LANES)
    units = own_w * tiles
    padded = tiles * LANES
    extra = 2 * (units - PLANE)
    has_extra = k // extra == core

    def place(u, half):
        return (u, half) if u < PLANE else (extra * core + 2 * (u - PLANE) + half, 2)

    def freq_peer(off):
        return (param, (q + off) % n_freq)

    def plane_peer(to):
        return (to * ring + z, q)

    def ring_peer(off):
        return (k * ring + (z + off) % ring, q)

    def remote(src, dst, ssem, rsem, to):
        return pltpu.make_async_remote_copy(
            src_ref=src, dst_ref=dst, send_sem=ssem, recv_sem=rsem, device_id=to, device_id_type=MESH
        )

    def signal(semaphore, to):
        pl.semaphore_signal(semaphore, inc=1, device_id=to, device_id_type=MESH)

    load_freq, load_mask, load_noise, load_prior, load_green = [
        pltpu.make_async_copy(src, dst, load_sem.at[i])
        for i, (src, dst) in enumerate(
            (
                (freq_hbm, freq_ref), (mask_hbm, mask_ref), (noise_hbm, noise_ref), (prior_hbm, prior_ref),
                (green_hbm, green),
            )
        )
    ]
    chunks = dir_sem.shape[0]
    size = times // chunks
    load_dirs = [
        pltpu.make_async_copy(dir_hbm.at[pl.ds(i * size, size)], dirs.at[pl.ds(i * size, size)], dir_sem.at[i])
        for i in range(chunks)
    ]
    for load in [load_freq] + load_dirs:
        load.start()

    y, x = k // ROW, k % ROW
    beside = [plane_peer(y * ROW + (x + 1) % ROW), plane_peer(y * ROW + (x + ROW - 1) % ROW)]
    across = [plane_peer((y + 1) % (PLANE // ROW) * ROW + x)]

    def along(d):
        return [ring_peer(d), ring_peer(ring - d)]

    barrier = pltpu.get_barrier_semaphore()
    peers = [freq_peer(o) for o in range(1, n_freq)] + beside + across + along(1)
    for peer in peers:
        signal(barrier, peer)
    rounds = [beside + across + along(1), beside + along(2), along(4)]

    def tell(i):
        for peer in rounds[i]:
            signal(near_sem.at[i], peer)

    def hear(i):
        pl.semaphore_wait(near_sem.at[i], len(rounds[i]))

    key = lax.broadcasted_iota(jnp.int32, (NF * pair, 1), 0)
    step = lax.broadcasted_iota(jnp.int32, (1, LANES), 1)
    row = lax.broadcasted_iota(jnp.int32, (NF * pair, size * RHS), 0)
    column = lax.broadcasted_iota(jnp.int32, (NF * pair, size * RHS), 1)
    same_side = row % RHS == column % RHS
    repeats = [jnp.where(row == column // RHS + i * size, 1.0, 0.0).astype(BF16) for i in range(chunks)]
    load_freq.wait()
    freq = jnp.zeros(key.shape, F32)
    for w in range(NF):
        freq = jnp.where(key // pair == w, freq_ref[w].astype(F32), freq)
    narrow = trig(freq, (key // RHS % 2).astype(F32), (step + q * times).astype(F32)).astype(BF16)
    tables = [
        jnp.where(same_side, jnp.dot(narrow, repeat, preferred_element_type=F32), 0.0).astype(BF16)
        for repeat in repeats
    ]
    part = jnp.zeros((NF * pair, columns), F32)
    for i in range(chunks):
        load_dirs[i].wait()
        steps = dirs[i * size : (i + 1) * size].astype(F32).reshape(size * RHS, columns).astype(BF16)
        part = part + jnp.dot(tables[i], steps, preferred_element_type=F32)
    for load in (load_mask, load_noise, load_green, load_prior):
        load.start()
    for g in range(n_freq):
        for w in range(own_w):
            piece = part[g * rows + w * pair : g * rows + (w + 1) * pair]
            spec_own[g, w] = piece
            spec_send[g, w] = piece.astype(BF16)

    pl.semaphore_wait(barrier, len(peers))
    far_freq = (2, 3, 1) if n_freq == 4 else tuple(range(1, n_freq))

    def spec_copy(w, off):
        return remote(
            spec_send.at[(q + off) % n_freq, w], spec_recv.at[off - 1, w],
            spec_ssem.at[w, off - 1], spec_rsem.at[w, off - 1], freq_peer(off),
        )

    for w in range(own_w):
        for off in far_freq:
            spec_copy(w, off).start()
    tell(0)

    load_mask.wait()
    sensor = lax.broadcasted_iota(jnp.int32, (padded, SBLK), 0)
    block = lax.broadcasted_iota(jnp.int32, (padded, SBLK), 1)
    per = SENSORS // SBLK
    picks = jnp.where((sensor >= block * per) & (sensor < (block + 1) * per), 1.0, 0.0).astype(BF16)
    block8 = lax.broadcasted_iota(jnp.int32, (SBLK, LANES), 0)
    parts = []
    for b in range(columns // PBLK):
        value = jnp.zeros((SBLK, LANES), F32)
        for s in range(SBLK):
            value = jnp.where(block8 == s, mask_ref[b, s].astype(F32), value)
        parts.append(value)
    blocks = jnp.concatenate(parts, axis=1).astype(BF16)
    mask[...] = jnp.dot(picks, blocks, preferred_element_type=F32).astype(BF16)
    load_green.wait()
    for w in range(own_w):
        for c in range(2):
            kern[w, c, :SENSORS, :] = green[w, c] * mask[:SENSORS, :]
            kern[w, c, SENSORS:, :] = jnp.zeros((padded - SENSORS, columns), BF16)
    hear(0)
    tell(1)
    for w in range(own_w):
        for c in range(2):
            turned[w, c] = kern[w, c].T
    load_noise.wait()
    noise[...] = jnp.zeros_like(noise)
    for u in range(units):
        w, j = u // tiles, u % tiles
        width = min(LANES, SENSORS - j * LANES)
        for half in range(2):
            row, part = place(u, half)
            noise[row, part, :, :width] = jnp.broadcast_to(
                noise_ref[w : w + 1, j * LANES : j * LANES + width], (RHS, width)
            )
    hear(1)
    tell(2)

    for w in range(own_w):
        first = spec_own[q, w]
        for off in far_freq:
            spec_copy(w, off).wait_recv()
            first = first + spec_recv[off - 1, w].astype(F32)
        second = jnp.concatenate([-first[RHS:], first[:RHS]], axis=0)
        data = jnp.dot(first.astype(BF16), turned[w, 0], preferred_element_type=F32) + jnp.dot(
            second.astype(BF16), turned[w, 1], preferred_element_type=F32
        )
        for j in range(tiles):
            for half in range(2):
                row, part = place(w * tiles + j, half)
                data_send[row, part] = data[half * RHS : (half + 1) * RHS, j * LANES : (j + 1) * LANES].astype(BF16)

    def data_copy(off, count):
        to, here = (k + off) % PLANE, pl.ds(0, count)
        return remote(
            data_send.at[to, here], data_recv.at[off, here], data_ssem.at[off], data_rsem.at[off], plane_peer(to)
        )

    def sum_copy(off, count):
        here = pl.ds(0, count)
        return remote(sum_send.at[here], sum_recv.at[off, here], sum_ssem.at[off], sum_rsem.at[off], ring_peer(off))

    def weighted_copy(off, count):
        own = weighted.at[k, pl.ds(0, count)]
        return remote(own, own, w_ssem.at[off], w_rsem.at[k], plane_peer((k + off) % PLANE))

    def weighted_arrival(owner, count):
        own = weighted.at[owner, pl.ds(0, count)]
        return remote(own, own, w_ssem.at[0], w_rsem.at[owner], plane_peer((k + 1) % PLANE))

    far_plane = [off for off in (6, 2, 5, 7, 3, 1, 4)]
    far_ring = sorted(range(1, ring), key=lambda off: -min(off, ring - off))

    for off in far_plane:
        two = (k + off) % PLANE // extra == core
        pl.when(two)(data_copy(off, 3).start)
        pl.when(jnp.logical_not(two))(data_copy(off, 2).start)

    for i in range(chunks):
        first_time = q * times + i * size
        back[i] = (2.0 * expanded_table(freq_ref, first_time, size * RHS, NF * pair, 1)).astype(BF16)
    load_prior.wait()
    for i in range(chunks):
        steps = dirs[i * size : (i + 1) * size].astype(F32).reshape(size * RHS, columns)
        damped[i] = steps * prior_ref[...]

    def reduce(count):
        acc = data_send[k, :count].astype(F32)
        for off in reversed(far_plane):
            data_copy(off, count).wait_recv()
            acc = acc + data_recv[off, :count].astype(F32)
        sum_send[:count] = acc.astype(BF16)
        hear(2)
        for off in far_ring:
            sum_copy(off, count).start()
        for off in reversed(far_ring):
            sum_copy(off, count).wait_recv()
            acc = acc + sum_recv[off, :count].astype(F32)
        weighted[k, :count] = (acc * noise[k, :count]).astype(BF16)
        for off in far_plane:
            weighted_copy(off, count).start()

    def finish(count):
        for off in far_ring:
            sum_copy(off, count).wait_send()
        for off in far_plane:
            weighted_copy(off, count).wait_send()

    pl.when(has_extra)(functools.partial(reduce, 3))
    pl.when(jnp.logical_not(has_extra))(functools.partial(reduce, 2))

    image_copies = []
    for w in range(own_w):
        for owner in range(PLANE) if w == 0 else ():
            two = owner // extra == core
            other = k != owner
            pl.when(jnp.logical_and(other, two))(weighted_arrival(owner, 3).wait_recv)
            pl.when(jnp.logical_and(other, jnp.logical_not(two)))(weighted_arrival(owner, 2).wait_recv)
        halves = [
            jnp.concatenate([weighted[place(w * tiles + j, half)].astype(F32) for j in range(tiles)], axis=1)
            for half in range(2)
        ]
        wide = jnp.concatenate(halves, axis=0)
        first = wide.astype(BF16)
        second = jnp.concatenate([halves[1], -halves[0]], axis=0).astype(BF16)
        image = jnp.dot(first, kern[w, 0], preferred_element_type=F32) + jnp.dot(
            second, kern[w, 1], preferred_element_type=F32
        )
        image = image.astype(BF16)
        image_send[w] = image
        images[q, w] = image
        for off in (2, 3, 1) if n_freq == 4 else range(1, n_freq):
            copy = remote(
                image_send.at[w], images.at[q, w], im_ssem.at[w, off - 1], im_rsem.at[w, off - 1], freq_peer(off)
            )
            copy.start()
            image_copies.append(copy)

    for w in range(own_w):
        for off in far_freq:
            spec_copy(w, off).wait_send()
    for off in far_plane:
        two = (k + off) % PLANE // extra == core
        pl.when(two)(data_copy(off, 3).wait_send)
        pl.when(jnp.logical_not(two))(data_copy(off, 2).wait_send)
    pl.when(has_extra)(functools.partial(finish, 3))
    pl.when(jnp.logical_not(has_extra))(functools.partial(finish, 2))
    for copy in image_copies:
        copy.wait_recv()
    every = images[...].reshape(NF * pair, columns)
    for i in range(chunks):
        summed = jnp.dot(back[i], every, preferred_element_type=F32)
        out_ref[i * size : (i + 1) * size] = (summed + damped[i]).reshape(size, RHS, columns).astype(BF16)
    for copy in image_copies:
        copy.wait_send()


def on_device(ring, n_freq, direction, green_blocks, block_mask, noise_weights, prior_precision, freq_index):
    times, _, columns = direction.shape
    own_w = NF // n_freq
    pair = 2 * RHS
    rows = own_w * pair
    keys = NF * pair
    tiles = -(-SENSORS // LANES)
    padded = tiles * LANES
    vmem = pltpu.VMEM
    dma = pltpu.SemaphoreType.DMA
    chunks = 3
    size = times // chunks
    operands = (
        direction, green_blocks, block_mask.T, noise_weights, freq_index, prior_precision.reshape(1, columns)
    )
    return pl.pallas_call(
        functools.partial(forward_kernel, ring, n_freq),
        out_shape=vmem(direction.shape, BF16),
        in_specs=[pl.BlockSpec(memory_space=pltpu.HBM)] * len(operands),
        out_specs=pl.BlockSpec(memory_space=vmem),
        scratch_shapes=[
            vmem((times, RHS, columns), BF16),
            vmem((own_w, 2, SENSORS, columns), BF16),
            pltpu.SMEM(block_mask.shape[::-1], jnp.int32),
            vmem((own_w, SENSORS), F32),
            pltpu.SMEM((NF,), jnp.int32),
            vmem((1, columns), F32),
            vmem((own_w, 2, padded, columns), BF16),
            vmem((own_w, 2, columns, padded), BF16),
            vmem((padded, columns), BF16),
            vmem((PLANE, 3, RHS, LANES), F32),
            vmem((n_freq, own_w, pair, columns), F32),
            vmem((n_freq, own_w, pair, columns), BF16),
            vmem((n_freq - 1, own_w, pair, columns), BF16),
            vmem((PLANE, 3, RHS, LANES), BF16),
            vmem((PLANE, 3, RHS, LANES), BF16),
            vmem((3, RHS, LANES), BF16),
            vmem((ring, 3, RHS, LANES), BF16),
            vmem((PLANE, 3, RHS, LANES), BF16),
            vmem((own_w, pair, columns), BF16),
            vmem((n_freq, own_w, pair, columns), BF16),
            vmem((chunks, size * RHS, keys), BF16),
            vmem((chunks, size * RHS, columns), F32),
            dma((5,)),
            dma((chunks,)),
            pltpu.SemaphoreType.REGULAR((3,)),
            dma((own_w, n_freq - 1)),
            dma((own_w, n_freq - 1)),
            dma((PLANE,)),
            dma((PLANE,)),
            dma((ring,)),
            dma((ring,)),
            dma((PLANE,)),
            dma((PLANE,)),
            dma((own_w, n_freq - 1)),
            dma((own_w, n_freq - 1)),
        ],
        compiler_params=pltpu.CompilerParams(
            collective_id=0, has_side_effects=True, vmem_limit_bytes=40 * 1024 * 1024
        ),
        name="forward",
    )(*(pltpu.with_memory_space_constraint(operand, pltpu.HBM) for operand in operands))


def solution(mesh):
    n_freq = mesh.shape["freq"]
    ring = mesh.shape["param"] // PLANE
    placed = (
        P("freq", None, "param"),
        P("freq", None, None, "param"),
        P(None, "param"),
        P("freq", None),
        P("param"),
        P(),
    )
    return jax.shard_map(
        functools.partial(on_device, ring, n_freq),
        mesh=mesh,
        in_specs=placed,
        out_specs=P("freq", None, "param"),
        check_vma=False,
    )
```
